256 devices in a mesh: ctx: 16 (over x, y), exp: 16 (over z, core).
Axes of the slice: x: 4, y: 4, z: 8, core: 2. Of those that a mesh axis runs over, the one named last changes fastest.
Arguments:
- residual_in: bfloat16 [4096, 4096], P(('ctx', 'exp')), may hold values from -6 to 6
- query_rows: bfloat16 [4096, 4096], P('ctx', 'exp'), may hold values from -6 to 6
- key_rows: bfloat16 [4096, 4096], P('ctx', 'exp'), may hold values from -6 to 6
- value_rows: bfloat16 [4096, 4096], P('ctx', 'exp'), may hold values from -6 to 6
- log_decay: float32 [4096, 32], P('ctx', 'exp'), may hold values from -3 to 0
- attn_gain: float32 [4096], P('exp'), may hold values from 0.5 to 1.5
- moe_gain: float32 [4096], replicated, may hold values from 0.5 to 1.5
- expert_ids: int32 [4096, 2], P(('ctx', 'exp')), may hold values from 0 to 15, all different within a row; in each aligned block of 16 rows (0 to 15, 16 to 31, ...) at most 3 rows name the same one
- route_weight: float32 [4096, 2], P(('ctx', 'exp')), may hold values from 0.1 to 1
- gate_weight: bfloat16 [16, 4096, 4608], P('exp', None, 'ctx'), may hold values from -0.09375 to 0.09375
- up_weight: bfloat16 [16, 4096, 4608], P('exp', None, 'ctx'), may hold values from -0.09375 to 0.09375
- down_weight: bfloat16 [16, 4608, 4096], P('exp', 'ctx'), may hold values from -0.09375 to 0.09375
Outputs:
- layer_out: bfloat16 [4096, 4096], P(('ctx', 'exp'))
The draws below stay inside these ranges and needn't reach their ends.
Inputs may be any that keep to these rules, and one draw needn't show every extreme that they name: `expert_ids`: each token names two different experts; in the rows of one device no expert is named by more than 3 tokens, a bound that some block reaches.
All inputs are finite; a program needn't handle non-finite values.
Results may differ from the reference program's by a relative error of at most 0.012.
Values may be sent and summed in bfloat16 or wider, within the bound.
A program may use at most 128 MiB of HBM per device.

```python
import math
import jax
import jax.numpy as jnp
import numpy as np
from jax import lax

HEAD = 128
HEADS = 32
D = 4096
FF = 4608
TOPK = 2
SPAN = 256
SEQUENCE_TOKENS = 4096
TOK_DEV = 16
EXPERTS = 16
CAP = 3
N_CTX = 16


def draw_log_decay(key, part):
    random_subkeys = jax.random.split(jax.random.fold_in(key, 17), 6)
    fast_share = 0.5
    choose = jax.random.uniform(random_subkeys[0], (HEADS,), jnp.float32)
    fast_rate = jnp.exp(jax.random.uniform(random_subkeys[1], (HEADS,), jnp.float32, math.log(1.0 / 50.0), math.log(1.0 / 30.0)))
    slow_rate = jnp.exp(jax.random.uniform(random_subkeys[2], (HEADS,), jnp.float32, math.log(0.05 / SEQUENCE_TOKENS), math.log(0.5 / SEQUENCE_TOKENS)))
    baseline_rate = jnp.where(choose < fast_share, fast_rate, slow_rate)
    coarse_noise = jax.random.uniform(random_subkeys[3], (SEQUENCE_TOKENS, HEADS), jnp.float32, 0.5, 1.5)
    spike_positions = jax.random.randint(random_subkeys[4], (4,), 0, SEQUENCE_TOKENS)
    spike_drops = jnp.log(jax.random.uniform(random_subkeys[5], (4,), jnp.float32, 0.5, 0.8))
    spike_hits = (jnp.arange(SEQUENCE_TOKENS)[:, None] == spike_positions[None, :]).astype(jnp.float32)
    spike_sum = jnp.sum(spike_hits * spike_drops[None, :], axis=1)
    return (spike_sum[:, None] - baseline_rate[None, :] * coarse_noise).astype(jnp.float32)


def levels(rng, dims, shards, smallest, largest):
    def one(axis_at, blocks):
        heights = jax.random.uniform(jax.random.fold_in(jax.random.fold_in(rng, 6), axis_at), (blocks,), jnp.float32, smallest / len(shards), largest / len(shards))
        return jnp.repeat(jnp.exp(heights), dims[axis_at] // blocks).reshape((-1,) + (1,) * (len(dims) - axis_at - 1))

    level = one(*shards[0])
    for cut in shards[1:]:
        level = level * one(*cut)
    return level


def shared_out(stream_key, own, number, rows, amount, top, reach, skew):
    sequence = jax.random.permutation(stream_key, amount)
    packed, common = shares(amount, rows * top, reach, skew, True), shares(amount, rows * top, reach, skew, False)
    places = jnp.arange(amount)

    def named(lengths, turn):
        used = int((lengths > 0).sum())
        fixed = max(1, used // 4)
        moved = fixed + (places - fixed + turn * (used - fixed)) % max(1, amount - fixed)
        return jnp.zeros((amount,), jnp.int32).at[sequence[jnp.where(places < fixed, places, moved)]].set(jnp.asarray(lengths, jnp.int32))

    lengths = jnp.where(number % 4 == 0, named(packed, number // 4), named(common, number - number // 4 - 1))
    mixed = jax.random.permutation(jax.random.fold_in(own, 3), amount)
    source_of, sink = mixed[0:amount // 2 * 2:2], mixed[1:amount // 2 * 2:2]
    room = jnp.minimum(lengths[source_of] - 1, reach - lengths[sink]) // 2
    room = jnp.where((source_of == sequence[0]) | (sink == sequence[0]) | (lengths[sink] == 0), 0, jnp.maximum(room, 0))
    moved = jax.random.randint(jax.random.fold_in(own, 4), (amount // 2,), 0, 1 << 20) % (room + 1)
    lengths = lengths.at[source_of].add(-moved).at[sink].add(moved)
    items = jnp.searchsorted(jnp.cumsum(lengths), jnp.arange(rows * top), side="right").astype(jnp.int32)
    table = items.reshape(top, rows).T
    table = table[jax.random.permutation(jax.random.fold_in(own, 1), rows)]
    turn = jax.random.randint(jax.random.fold_in(own, 2), (rows, 1), 0, top)
    return jnp.take_along_axis(table, (jnp.arange(top)[None, :] + turn) % top, axis=1)


def shares(amount, total, reach, lean, full):
    loads = [(1 << 20) // math.isqrt(standing ** lean) + 1 for standing in range(1, amount + 1)]
    largest = reach if full else min(reach, max(-(-total // amount), total * loads[0] // sum(loads)))
    least = 1 if total - largest >= amount - 1 else 0
    counts, spare = [largest] + [least] * (amount - 1), total - largest - least * (amount - 1)
    while spare > 0:
        free = [i for i in range(1, amount) if counts[i] < largest] or [i for i in range(1, amount) if counts[i] < reach]
        pool, left = sum([loads[i] for i in free]), spare
        for i in free:
            extra = min(reach - counts[i], max(1, left * loads[i] // pool), spare)
            counts[i] = counts[i] + extra
            spare = spare - extra
    return np.array(counts)


def gaussian(own_key, dims, scale, limit, shards=(), kind=jnp.bfloat16):
    factor_of = levels(own_key, dims, shards, -0.22, 0.18) if shards else 1.0
    values = jax.random.normal(own_key, dims, jnp.float32) * scale * factor_of
    return jnp.minimum(jnp.maximum(values, -limit), limit).astype(kind)


def setup_inputs(seed: int = 0) -> dict:
    keys = jax.random.split(jax.random.key(seed), 13)
    residual_in = gaussian(keys[0], (SEQUENCE_TOKENS, D), 1.0, 6.0, ((0, 256),))
    query_rows = gaussian(keys[1], (SEQUENCE_TOKENS, D), 1.0, 6.0, ((0, 16), (1, 16)))
    key_rows = gaussian(keys[2], (SEQUENCE_TOKENS, D), 1.0, 6.0, ((0, 16), (1, 16)))
    value_rows = gaussian(keys[3], (SEQUENCE_TOKENS, D), 1.0, 6.0, ((0, 16), (1, 16)))
    log_decay = draw_log_decay(jax.random.fold_in(keys[12], 71), 0)
    attn_gain = jnp.clip(1.0 + 0.1 * jax.random.normal(keys[5], (D,), jnp.float32), 0.5, 1.5)
    moe_gain = jnp.clip(1.0 + 0.1 * jax.random.normal(keys[6], (D,), jnp.float32), 0.5, 1.5)
    expert_ids_keys = jax.random.split(jax.random.fold_in(keys[7], 1), SEQUENCE_TOKENS // TOK_DEV)
    expert_ids_turns = jax.random.permutation(jax.random.fold_in(keys[7], 3), SEQUENCE_TOKENS // TOK_DEV)
    expert_ids = jax.vmap(lambda own, number: shared_out(jax.random.fold_in(keys[7], 2), own, number, TOK_DEV, EXPERTS, TOPK, CAP, 2))(expert_ids_keys, expert_ids_turns).reshape((SEQUENCE_TOKENS, TOPK))
    route_weight = jnp.clip(0.1 + 0.9 * jax.random.uniform(keys[8], (SEQUENCE_TOKENS, TOPK), jnp.float32) ** levels(keys[8], (SEQUENCE_TOKENS, TOPK), ((0, 256),), -0.2, 0.2), 0.1, 1.0)
    gate_weight = gaussian(keys[9], (EXPERTS, D, FF), D ** -0.5, 0.09375, ((0, 16), (2, 16)))
    up_weight = gaussian(keys[10], (EXPERTS, D, FF), D ** -0.5, 0.09375, ((0, 16), (2, 16)))
    down_weight = gaussian(keys[11], (EXPERTS, FF, D), FF ** -0.5, 0.09375, ((0, 16), (1, 16)))
    return {"residual_in": residual_in, "query_rows": query_rows, "key_rows": key_rows, "value_rows": value_rows, "log_decay": log_decay, "attn_gain": attn_gain, "moe_gain": moe_gain, "expert_ids": expert_ids, "route_weight": route_weight, "gate_weight": gate_weight, "up_weight": up_weight, "down_weight": down_weight}


EPSILON = 1e-05

def round_bf16(tensor):
    return lax.optimization_barrier(tensor.astype(jnp.bfloat16)).astype(jnp.float32)

def attention_block(state, block):
    query_blk, key_blk, value_blk, decay_blk = block
    query_f = query_blk.astype(jnp.float32)
    key_f = key_blk.astype(jnp.float32)
    value_f = value_blk.astype(jnp.float32)
    cumulative = jnp.cumsum(decay_blk, axis=0)
    block_total = cumulative[-1]
    length = decay_blk.shape[0]
    causal = jnp.arange(length)[:, None] >= jnp.arange(length)[None, :]
    spread = cumulative.T[:, :, None] - cumulative.T[:, None, :]
    decay_mask = jnp.exp(jnp.where(causal[None], spread, -jnp.inf))
    scores = jnp.einsum('thd,shd->hts', query_f, key_f)
    attend_weight = round_bf16(scores * decay_mask)
    within = jnp.einsum('hts,shd->thd', attend_weight, value_f)
    carried = jnp.exp(cumulative)[:, :, None] * jnp.einsum('thd,hde->the', query_f, round_bf16(state))
    weighted = round_bf16(key_f * jnp.exp(block_total - cumulative)[:, :, None])
    update = jnp.einsum('thd,the->hde', weighted, value_f)
    new_state = jnp.exp(block_total)[:, None, None] * state + update
    return (new_state, carried + within)

def expert_apply(operands):
    rows_in, gate_mat, up_mat, down_mat = operands
    slice_width = FF // N_CTX
    gate_slices = gate_mat.reshape(D, N_CTX, slice_width).transpose(1, 0, 2)
    up_slices = up_mat.reshape(D, N_CTX, slice_width).transpose(1, 0, 2)
    down_slices = down_mat.reshape(N_CTX, slice_width, D)

    def add_slice(running, slices):
        gate_val = jnp.dot(rows_in, slices[0], preferred_element_type=jnp.float32)
        up_val = jnp.dot(rows_in, slices[1], preferred_element_type=jnp.float32)
        hidden_act = (jax.nn.silu(gate_val) * up_val).astype(jnp.bfloat16)
        slice_part = round_bf16(jnp.dot(hidden_act, slices[2], preferred_element_type=jnp.float32))
        return (running + slice_part, None)
    start_sum = jnp.zeros((rows_in.shape[0], D), jnp.float32)
    summed, _ = lax.scan(add_slice, start_sum, (gate_slices, up_slices, down_slices))
    return summed.astype(jnp.bfloat16)

def reference(residual_in, query_rows, key_rows, value_rows, log_decay, attn_gain, moe_gain, expert_ids, route_weight, gate_weight, up_weight, down_weight):
    blocks = SEQUENCE_TOKENS // SPAN
    block_shape = (blocks, SPAN, HEADS, HEAD)
    start_state = jnp.zeros((HEADS, HEAD, HEAD), jnp.float32)
    _, raw_out = lax.scan(attention_block, start_state, (query_rows.reshape(block_shape), key_rows.reshape(block_shape), value_rows.reshape(block_shape), log_decay.reshape(blocks, SPAN, HEADS)))
    raw_out = raw_out.reshape(SEQUENCE_TOKENS, HEADS, HEAD)
    scale_rms = lax.rsqrt(lax.optimization_barrier(jnp.mean(raw_out * raw_out, axis=-1, keepdims=True)) + EPSILON)
    head_out = (raw_out * scale_rms * attn_gain.reshape(HEADS, HEAD)).astype(jnp.bfloat16).reshape(SEQUENCE_TOKENS, D)
    hidden_state = residual_in.astype(jnp.float32) + head_out.astype(jnp.float32)
    normed = (hidden_state * lax.rsqrt(lax.optimization_barrier(jnp.mean(hidden_state * hidden_state, axis=-1, keepdims=True)) + EPSILON) * moe_gain).astype(jnp.bfloat16)
    groups = SEQUENCE_TOKENS // TOK_DEV
    pair_count = TOK_DEV * TOPK
    flat_ids = expert_ids.reshape(groups, pair_count).astype(jnp.int32)
    one_hot = (flat_ids[:, :, None] == jnp.arange(EXPERTS, dtype=jnp.int32)[None, None, :]).astype(jnp.int32)
    before = jnp.cumsum(one_hot, axis=1) - one_hot
    slot_index = lax.optimization_barrier(jnp.sum(before * one_hot, axis=2))
    target = (flat_ids * CAP + slot_index).astype(jnp.int32)
    pair_rows = jnp.broadcast_to(normed.reshape(groups, TOK_DEV, 1, D), (groups, TOK_DEV, TOPK, D)).reshape(groups, pair_count, D)
    owner = jnp.broadcast_to(jnp.arange(groups, dtype=jnp.int32)[:, None], (groups, pair_count))
    buffer = jnp.zeros((groups, EXPERTS * CAP, D), normed.dtype).at[owner, target].set(pair_rows)
    per_expert = buffer.reshape(groups, EXPERTS, CAP, D).transpose(1, 0, 2, 3).reshape(EXPERTS, groups * CAP, D)
    expert_out = lax.map(expert_apply, (per_expert, gate_weight, up_weight, down_weight))
    returned_rows = expert_out.reshape(EXPERTS, groups, CAP, D).transpose(1, 0, 2, 3).reshape(groups, EXPERTS * CAP, D)
    picked = jnp.take_along_axis(returned_rows, target[:, :, None], axis=1).astype(jnp.float32)
    picked = picked.reshape(SEQUENCE_TOKENS, TOPK, D)
    contrib = lax.optimization_barrier(jnp.sum(picked * route_weight[:, :, None], axis=1))
    return (hidden_state + contrib).astype(jnp.bfloat16)
```

```python
import functools

import jax
import jax.numpy as jnp
from jax import lax
from jax.experimental import pallas as pl
from jax.experimental.pallas import tpu as pltpu
from jax.sharding import PartitionSpec as P

HEAD = 128
EPSILON = 1e-05
RING = 4
SLOTS = 3
F32 = jnp.float32
BF16 = jnp.bfloat16
HIGHEST = lax.Precision.HIGHEST
MESH = pl.DeviceIdType.MESH


def iota(shape, dim):
    return lax.broadcasted_iota(jnp.int32, shape, dim)


def dot(a, b, dims=((1,), (0,)), precision=None):
    return lax.dot_general(
        a, b, (dims, ((), ())), precision=precision, preferred_element_type=F32
    )


def one(condition):
    return jnp.where(condition, 1.0, 0.0).astype(F32)


def layer_kernel(
    experts,
    residual_ref,
    query_ref,
    key_ref,
    value_ref,
    decay_ref,
    attn_gain_ref,
    moe_gain_ref,
    ids_ref,
    route_ref,
    gate_ref,
    up_ref,
    down_ref,
    out_ref,
    state_buf,
    total_buf,
    row_buf,
    row_total_buf,
    within,
    head_out,
    head_recv,
    hidden,
    pick,
    comb,
    packed,
    arrived,
    gathered,
    partial,
    opp1,
    fin1,
    opp2,
    fin2,
    back,
    returned,
    gu_weight,
    down_weight,
    weight_sem,
    state_send,
    state_recv,
    head_sem,
    dispatch_send,
    dispatch_recv,
    return_send,
    return_recv,
    ag_send,
    ag_recv,
    rs_send,
    rs_recv,
):
    length = query_ref.shape[0]
    width = query_ref.shape[1]
    heads = width // HEAD
    tokens = residual_ref.shape[0]
    model = residual_ref.shape[1]
    hid = down_ref.shape[1]
    main = hid // 256 * 256 if hid >= 256 else hid
    half = model // 2
    quarter = model // 4

    ctx = lax.axis_index("ctx")
    exp = lax.axis_index("exp")
    row, col = ctx // RING, lax.rem(ctx, RING)

    def along_x(step):
        return {"ctx": lax.rem(row + step, RING) * RING + col}

    def along_y(step):
        return {"ctx": row * RING + lax.rem(col + step, RING)}

    def along_exp(step):
        return {"exp": lax.rem(exp + step, experts)}

    def remote(src, dst, send, recv, device):
        return pltpu.make_async_remote_copy(
            src_ref=src,
            dst_ref=dst,
            send_sem=send,
            recv_sem=recv,
            device_id=device,
            device_id_type=MESH,
        )

    barrier = pltpu.get_barrier_semaphore()
    for step in range(1, RING):
        pl.semaphore_signal(barrier, inc=1, device_id=along_x(step), device_id_type=MESH)
        pl.semaphore_signal(barrier, inc=1, device_id=along_y(step), device_id_type=MESH)
    for step in range(1, experts):
        pl.semaphore_signal(barrier, inc=1, device_id=along_exp(step), device_id_type=MESH)

    weights = [
        pltpu.make_async_copy(gate_ref, gu_weight.at[0:hid], weight_sem.at[0]),
        pltpu.make_async_copy(up_ref, gu_weight.at[hid : 2 * hid], weight_sem.at[1]),
        pltpu.make_async_copy(down_ref.at[0], down_weight, weight_sem.at[2]),
    ]
    for copy in weights:
        copy.start()

    r = iota((length, length), 0)
    c = iota((length, length), 1)
    causal = r >= c
    decay = decay_ref[...]
    cum = dot(one(causal), decay, ((1,), (1,)), HIGHEST)
    cum_t = dot(decay, one(r <= c), precision=HIGHEST)
    totals = [cum_t[h : h + 1, length - 1 : length] for h in range(heads)]
    updates = []
    for h in range(heads):
        lanes = slice(h * HEAD, (h + 1) * HEAD)
        scaled = key_ref[:, lanes].astype(F32) * jnp.exp(totals[h] - cum[:, h : h + 1])
        update = dot(scaled.astype(BF16), value_ref[:, lanes], ((0,), (0,)))
        updates.append(update)
        state_buf[0, lanes, :] = update.astype(BF16)
        total_buf[0, 8 * h : 8 * h + 8, :] = jnp.broadcast_to(totals[h], (8, HEAD))

    pl.semaphore_wait(barrier, 2 * (RING - 1) + experts - 1)

    def exchange(states, sums, base, neighbour):
        copies = []
        for step in range(1, RING):
            slot, k = RING - step, base + 2 * (step - 1)
            to = neighbour(step)
            copies.append(
                remote(states.at[0], states.at[slot], state_send.at[k], state_recv.at[k], to)
            )
            copies.append(
                remote(sums.at[0], sums.at[slot], state_send.at[k + 1], state_recv.at[k + 1], to)
            )
        for copy in copies:
            copy.start()
        return copies

    stage1 = exchange(state_buf, total_buf, 0, along_y)

    for h in range(heads):
        lanes = slice(h * HEAD, (h + 1) * HEAD)
        spread = cum[:, h : h + 1] - cum_t[h : h + 1, :]
        mask = jnp.exp(jnp.where(causal, spread, -jnp.inf))
        scores = dot(query_ref[:, lanes], key_ref[:, lanes], ((1,), (1,)))
        within[:, lanes] = dot((scores * mask).astype(BF16), value_ref[:, lanes])

    for copy in stage1:
        copy.wait_recv()

    def earlier(states, sums, h, position):
        lanes = slice(h * HEAD, (h + 1) * HEAD)
        state = jnp.zeros((HEAD, HEAD), F32)
        passed = jnp.zeros((1, HEAD), F32)
        for back_by in range(1, RING):
            slot = RING - back_by
            valid = position >= back_by
            state = state + jnp.where(
                valid, jnp.exp(passed) * states[slot, lanes, :].astype(F32), 0.0
            )
            passed = passed + jnp.where(valid, sums[slot, 8 * h : 8 * h + 1, :], 0.0)
        return state, passed

    before_row = []
    for h in range(heads):
        lanes = slice(h * HEAD, (h + 1) * HEAD)
        state, passed = earlier(state_buf, total_buf, h, col)
        before_row.append((state, passed))
        total = total_buf[0, 8 * h : 8 * h + 1, :]
        whole = jnp.exp(total) * state + updates[h]
        whole_total = passed + total
        for step in range(1, RING):
            valid = col + step < RING
            next_total = jnp.where(valid, total_buf[step, 8 * h : 8 * h + 1, :], 0.0)
            whole = jnp.exp(next_total) * whole + jnp.where(
                valid, state_buf[step, lanes, :].astype(F32), 0.0
            )
            whole_total = whole_total + next_total
        row_buf[0, lanes, :] = whole.astype(BF16)
        row_total_buf[0, 8 * h : 8 * h + 8, :] = jnp.broadcast_to(whole_total, (8, HEAD))
    stage2 = exchange(row_buf, row_total_buf, 2 * (RING - 1), along_x)

    block = experts * tokens
    tok_r, tok_c = iota((tokens, tokens), 0), iota((tokens, tokens), 1)
    rel = lax.rem(ids_ref[...] - exp + experts, experts)
    oh0 = one(iota((experts, tokens), 0) == rel[0:1, :])
    oh1 = one(iota((experts, tokens), 0) == rel[1:2, :])
    count0 = dot((oh0 + oh1).astype(BF16), one(tok_r < tok_c).astype(BF16))
    count1 = count0 + oh0
    by_high = one(iota((block, experts), 0) // tokens == iota((block, experts), 1)).astype(BF16)
    by_low = one(lax.rem(iota((block, tokens), 0), tokens) == iota((block, tokens), 1)).astype(BF16)
    swap = (iota((block, block), 0) // tokens == lax.rem(iota((block, block), 1), tokens))
    same = lax.rem(iota((block, block), 0), tokens) == iota((block, block), 1) // tokens
    turn = one(jnp.logical_and(swap, same)).astype(BF16)
    for s in range(SLOTS):
        take0 = oh0 * one(count0 == s)
        take1 = oh1 * one(count1 == s)
        chosen = dot(by_high, (take0 + take1).astype(BF16)).astype(BF16)
        chosen = dot(chosen, by_low, ((1,), (1,)))
        pick[s] = jnp.where(same, chosen, 0.0).astype(BF16)
        weight = route_ref[0:1, :] * take0 + route_ref[1:2, :] * take1
        high = weight.astype(BF16)
        low = (weight - high.astype(F32)).astype(BF16)
        for part, piece in enumerate((high, low)):
            spread_out = dot(by_low, piece, ((1,), (1,))).astype(BF16)
            spread_out = dot(spread_out, by_high, ((1,), (1,)))
            comb[s, part] = jnp.where(swap, spread_out, 0.0).astype(BF16)

    for copy in stage2:
        copy.wait_recv()

    for h in range(heads):
        lanes = slice(h * HEAD, (h + 1) * HEAD)
        state, passed = before_row[h]
        rows_state, _ = earlier(row_buf, row_total_buf, h, row)
        incoming = state + jnp.exp(passed) * rows_state
        carried = dot(query_ref[:, lanes], incoming.astype(BF16))
        raw = jnp.exp(cum[:, h : h + 1]) * carried + within[:, lanes]
        scale = lax.rsqrt(jnp.mean(raw * raw, axis=-1, keepdims=True) + EPSILON)
        head_out[:, lanes] = (raw * scale * attn_gain_ref[:, lanes]).astype(BF16)

    def token_rows(device):
        return head_out.at[pl.ds(pl.multiple_of(device * tokens, tokens), tokens), :]

    head_copies = []
    for step in range(1, experts):
        to = along_exp(step)
        head_copies.append(
            remote(token_rows(to["exp"]), head_recv.at[exp], head_sem.at[0], head_sem.at[1], to)
        )
    for copy in head_copies:
        copy.start()
    own = pltpu.make_async_copy(token_rows(exp), head_recv.at[exp], head_sem.at[1])
    own.start()
    pltpu.make_async_copy(head_recv, head_recv, head_sem.at[1]).wait()

    squares = jnp.zeros((tokens, 1), F32)
    for j in range(experts):
        lanes = slice(j * width, (j + 1) * width)
        rows = slice(j * tokens, (j + 1) * tokens)
        value = residual_ref[:, lanes].astype(F32) + head_recv[j].astype(F32)
        hidden[rows, :] = value
        squares = squares + jnp.sum(value * value, axis=-1, keepdims=True)
    scale = lax.rsqrt(squares / model + EPSILON)
    normed = jnp.concatenate(
        [
            (
                hidden[j * tokens : (j + 1) * tokens, :]
                * scale
                * moe_gain_ref[:, j * width : (j + 1) * width]
            ).astype(BF16)
            for j in range(experts)
        ],
        axis=0,
    )

    def cross(source, target, send, recv):
        copies = [
            remote(source.at[step], target.at[experts - step], send, recv, along_exp(step))
            for step in range(1, experts)
        ]
        for copy in copies:
            copy.start()
        own_block = pltpu.make_async_copy(source.at[0], target.at[0], recv)
        own_block.start()

    for s in range(SLOTS):
        packed[s] = dot(pick[s], normed).astype(BF16).reshape(experts, tokens, width)
        cross(packed.at[s], arrived.at[s], dispatch_send.at[s], dispatch_recv.at[s])

    def take_rows(s):
        pltpu.make_async_copy(arrived.at[s], arrived.at[s], dispatch_recv.at[s]).wait()
        turned = dot(turn, arrived[s].reshape(block, width)).astype(BF16)
        for j in range(experts):
            gathered[s, 0, 0, :, j * width : (j + 1) * width] = turned[
                j * tokens : (j + 1) * tokens, :
            ]

    def columns(n, part=None):
        if part is None:
            return slice(n * half, (n + 1) * half)
        start = n * half + part * quarter
        return slice(start, start + quarter)

    def gather_ring(s, phase, n):
        on_x = (phase == 0) == (n == 0)
        step_by = along_x if on_x else along_y

        def view(part, slot):
            if phase == 0:
                at = (slot, 0) if on_x else (0, slot)
                return gathered.at[s, at[0], at[1], :, columns(n, part)]
            two = slice(2 * part, 2 * part + 2)
            if on_x:
                return gathered.at[s, slot, two, :, columns(n)]
            return gathered.at[s, two, slot, :, columns(n)]

        k = (s * 2 + phase) * 2 + n

        def make(i, part, source, target, step):
            return remote(
                view(part, source), view(part, target), ag_send.at[k, i], ag_recv.at[k, i],
                step_by(step),
            )

        return [
            make(0, 0, 0, 3, 1),
            make(1, 1, 0, 1, 3),
            make(2, 1, 0, 3, 1),
            make(3, 0, 0, 1, 3),
            make(4, 0, 3, 2, 1),
            make(5, 1, 1, 2, 3),
        ]

    gathers = {
        (s, phase): [gather_ring(s, phase, n) for n in range(2)]
        for s in range(SLOTS)
        for phase in range(2)
    }

    def gather_start(s, phase):
        for i in range(4):
            for ring in gathers[s, phase]:
                ring[i].start()

    def gather_forward(s, phase):
        for i in range(2):
            for ring in gathers[s, phase]:
                ring[i].wait_recv()
                ring[4 + i].start()

    def gather_finish(s, phase):
        for i in range(2, 6):
            for ring in gathers[s, phase]:
                ring[i].wait_recv()

    def sum_ring(s, phase, n):
        on_x = (phase == 0) == (n == 1)
        step_by = along_x if on_x else along_y

        def own_view(part, slot):
            if phase == 0:
                two = slice(2 * part, 2 * part + 2)
                if on_x:
                    return partial.at[s, slot, two, :, columns(n)]
                return partial.at[s, two, slot, :, columns(n)]
            at = (slot, 0) if on_x else (0, slot)
            return partial.at[s, at[0], at[1], :, columns(n, part)]

        def opposite(part):
            if phase == 0:
                return opp1.at[s, n, part]
            return opp2.at[s, n, part]

        def final(side, part):
            if phase == 0:
                return fin1.at[s, n, side, 2 * part : 2 * part + 2]
            return fin2.at[s, n, side, :, part * quarter : (part + 1) * quarter]

        k = (s * 2 + phase) * 2 + n

        def make(i, source, target, step):
            return remote(source, target, rs_send.at[k, i], rs_recv.at[k, i], step_by(step))

        copies = [
            make(0, own_view(0, 2), opposite(0), 1),
            make(1, own_view(1, 2), opposite(1), 3),
            make(2, own_view(1, 1), final(0, 1), 1),
            make(3, own_view(0, 3), final(1, 0), 3),
            make(4, own_view(0, 1), final(0, 0), 1),
            make(5, own_view(1, 3), final(1, 1), 3),
        ]
        return copies, own_view, opposite, final

    sums = {
        (s, phase): [sum_ring(s, phase, n) for n in range(2)]
        for s in range(SLOTS)
        for phase in range(2)
    }

    def sum_start(s, phase):
        for i in range(4):
            for copies, _, _, _ in sums[s, phase]:
                copies[i].start()

    def sum_forward(s, phase):
        for part, slot in ((0, 1), (1, 3)):
            for copies, own_view, opposite, _ in sums[s, phase]:
                copies[part].wait_recv()
                mine = own_view(part, slot)
                mine[...] = (mine[...].astype(F32) + opposite(part)[...].astype(F32)).astype(BF16)
                copies[4 + part].start()

    def sum_finish(s, phase):
        for copies, own_view, _, final in sums[s, phase]:
            for i in range(2, 6):
                copies[i].wait_recv()
            for part in range(2):
                mine = own_view(part, 0)
                mine[...] = (
                    mine[...].astype(F32)
                    + final(0, part)[...].astype(F32)
                    + final(1, part)[...].astype(F32)
                ).astype(BF16)

    def give_back(s):
        rows = jnp.concatenate(
            [partial[s, 0, 0, :, j * width : (j + 1) * width] for j in range(experts)], axis=0
        )
        back[s] = dot(turn, rows).astype(BF16).reshape(experts, tokens, width)
        cross(back.at[s], returned.at[s], return_send.at[s], return_recv.at[s])

    many = RING * RING * tokens

    def expert_in(s):
        rows = gathered[s].reshape(many, model)
        both = dot(gu_weight[...], rows, ((1,), (1,)))
        act = jax.nn.silu(both[0:hid]) * both[hid : 2 * hid]
        return act.astype(BF16)

    def expert_out(s, act):
        for piece in range(4):
            lanes = slice(piece * quarter, (piece + 1) * quarter)
            made = dot(act, down_weight[:, lanes], ((0,), (0,)))
            partial[s, :, :, :, lanes] = made.astype(BF16).reshape(RING, RING, tokens, quarter)

    take_rows(0)
    gather_start(0, 0)
    take_rows(1)
    gather_forward(0, 0)
    gather_start(1, 0)
    gather_finish(0, 0)
    gather_start(0, 1)
    take_rows(2)
    gather_forward(1, 0)
    gather_forward(0, 1)
    gather_finish(1, 0)
    gather_start(1, 1)
    gather_start(2, 0)
    gather_finish(0, 1)
    for copy in weights:
        copy.wait()
    act = expert_in(0)
    gather_forward(1, 1)
    gather_forward(2, 0)
    gather_finish(2, 0)
    gather_start(2, 1)
    expert_out(0, act)
    sum_start(0, 0)
    gather_finish(1, 1)
    act = expert_in(1)
    gather_forward(2, 1)
    sum_forward(0, 0)
    expert_out(1, act)
    sum_start(1, 0)
    gather_finish(2, 1)
    sum_finish(0, 0)
    sum_start(0, 1)
    act = expert_in(2)
    sum_forward(1, 0)
    sum_forward(0, 1)
    expert_out(2, act)
    sum_start(2, 0)
    sum_finish(0, 1)
    give_back(0)
    sum_finish(1, 0)
    sum_start(1, 1)
    sum_forward(2, 0)
    sum_forward(1, 1)
    sum_finish(1, 1)
    give_back(1)
    sum_finish(2, 0)
    sum_start(2, 1)
    sum_forward(2, 1)
    sum_finish(2, 1)
    give_back(2)

    for s in range(SLOTS):
        pltpu.make_async_copy(returned.at[s], returned.at[s], return_recv.at[s]).wait()
        rows = returned[s].reshape(block, width)
        hidden[...] += dot(comb[s, 0], rows) + dot(comb[s, 1], rows)
    for j in range(experts):
        out_ref[:, j * width : (j + 1) * width] = hidden[
            j * tokens : (j + 1) * tokens, :
        ].astype(BF16)

    for copy in stage1 + stage2:
        copy.wait_send()
    sent = head_recv.at[1:]
    pltpu.make_async_copy(sent, sent, head_sem.at[0]).wait()
    for s in range(SLOTS):
        sent = arrived.at[s, 1:]
        pltpu.make_async_copy(sent, sent, dispatch_send.at[s]).wait()
        sent = returned.at[s, 1:]
        pltpu.make_async_copy(sent, sent, return_send.at[s]).wait()
    for rings in gathers.values():
        for ring in rings:
            for copy in ring:
                copy.wait_send()
    for rings in sums.values():
        for ring in rings:
            for copy in ring[0]:
                copy.wait_send()


def body(
    residual_in,
    query_rows,
    key_rows,
    value_rows,
    log_decay,
    attn_gain,
    moe_gain,
    expert_ids,
    route_weight,
    gate_weight,
    up_weight,
    down_weight,
):
    experts = lax.axis_size("exp")
    tokens, model = residual_in.shape
    length, width = query_rows.shape
    heads = width // HEAD
    hid = down_weight.shape[1]
    half, quarter = model // 2, model // 4
    block = experts * tokens
    dma = pltpu.SemaphoreType.DMA
    vmem = pl.BlockSpec(memory_space=pltpu.VMEM)
    hbm = pl.BlockSpec(memory_space=pl.ANY)
    return pl.pallas_call(
        functools.partial(layer_kernel, experts),
        out_shape=jax.ShapeDtypeStruct((tokens, model), BF16),
        in_specs=[vmem] * 9 + [hbm] * 3,
        out_specs=vmem,
        scratch_shapes=[
            pltpu.VMEM((RING, width, HEAD), BF16),
            pltpu.VMEM((RING, 8 * heads, HEAD), F32),
            pltpu.VMEM((RING, width, HEAD), BF16),
            pltpu.VMEM((RING, 8 * heads, HEAD), F32),
            pltpu.VMEM((length, width), F32),
            pltpu.VMEM((length, width), BF16),
            pltpu.VMEM((experts, tokens, width), BF16),
            pltpu.VMEM((block, width), F32),
            pltpu.VMEM((SLOTS, block, block), BF16),
            pltpu.VMEM((SLOTS, 2, block, block), BF16),
            pltpu.VMEM((SLOTS, experts, tokens, width), BF16),
            pltpu.VMEM((SLOTS, experts, tokens, width), BF16),
            pltpu.VMEM((SLOTS, RING, RING, tokens, model), BF16),
            pltpu.VMEM((SLOTS, RING, RING, tokens, model), BF16),
            pltpu.VMEM((SLOTS, 2, 2, 2, tokens, half), BF16),
            pltpu.VMEM((SLOTS, 2, 2, RING, tokens, half), BF16),
            pltpu.VMEM((SLOTS, 2, 2, tokens, quarter), BF16),
            pltpu.VMEM((SLOTS, 2, 2, tokens, half), BF16),
            pltpu.VMEM((SLOTS, experts, tokens, width), BF16),
            pltpu.VMEM((SLOTS, experts, tokens, width), BF16),
            pltpu.VMEM((2 * hid, model), BF16),
            pltpu.VMEM((hid, model), BF16),
            dma((3,)),
            dma((4 * (RING - 1),)),
            dma((4 * (RING - 1),)),
            dma((2,)),
            dma((SLOTS,)),
            dma((SLOTS,)),
            dma((SLOTS,)),
            dma((SLOTS,)),
            dma((4 * SLOTS, 6)),
            dma((4 * SLOTS, 6)),
            dma((4 * SLOTS, 6)),
            dma((4 * SLOTS, 6)),
        ],
        compiler_params=pltpu.CompilerParams(
            collective_id=0, has_side_effects=True, vmem_limit_bytes=56 * 1024 * 1024
        ),
    )(
        residual_in,
        query_rows,
        key_rows,
        value_rows,
        log_decay.T,
        attn_gain.reshape(1, -1),
        moe_gain.reshape(1, -1),
        expert_ids.T,
        route_weight.T,
        gate_weight[0].T,
        up_weight[0].T,
        down_weight,
    )


def solution(mesh):
    in_specs = (
        P(("ctx", "exp"), None),
        P("ctx", "exp"),
        P("ctx", "exp"),
        P("ctx", "exp"),
        P("ctx", "exp"),
        P("exp"),
        P(),
        P(("ctx", "exp"), None),
        P(("ctx", "exp"), None),
        P("exp", None, "ctx"),
        P("exp", None, "ctx"),
        P("exp", "ctx", None),
    )
    out_specs = P(("ctx", "exp"), None)
    return jax.shard_map(body, mesh=mesh, in_specs=in_specs, out_specs=out_specs, check_vma=False)
```

```python
import functools

import jax
import jax.numpy as jnp
from jax import lax
from jax.experimental import pallas as pl
from jax.experimental.pallas import tpu as pltpu
from jax.sharding import PartitionSpec as P

HEAD = 128
EPSILON = 1e-05
RING = 4
SLOTS = 3
DIRECT_GATHER = (0,)
DIRECT_SUM = (2,)
F32 = jnp.float32
BF16 = jnp.bfloat16
HIGHEST = lax.Precision.HIGHEST
MESH = pl.DeviceIdType.MESH


def iota(shape, dim):
    return lax.broadcasted_iota(jnp.int32, shape, dim)


def dot(a, b, dims=((1,), (0,)), precision=None):
    return lax.dot_general(
        a, b, (dims, ((), ())), precision=precision, preferred_element_type=F32
    )


def one(condition):
    return jnp.where(condition, 1.0, 0.0).astype(F32)


def layer_kernel(
    experts,
    residual_hbm,
    query_hbm,
    key_hbm,
    value_hbm,
    decay_hbm,
    attn_gain_hbm,
    moe_gain_hbm,
    ids_hbm,
    route_hbm,
    gate_ref,
    up_ref,
    down_ref,
    out_ref,
    residual_ref,
    query_ref,
    key_ref,
    value_ref,
    decay_ref,
    attn_gain_ref,
    moe_gain_ref,
    ids_ref,
    route_ref,
    total_buf,
    state_buf,
    message,
    message_in,
    within,
    head_out,
    head_recv,
    hidden,
    taken,
    comb,
    packed_res,
    arrived_res,
    packed,
    arrived,
    gathered,
    partial,
    opp1,
    fin1,
    opp2,
    fin2,
    fin_direct,
    back,
    returned,
    gu_weight,
    down_weight,
    input_sem,
    weight_sem,
    total_sem,
    taken_sem,
    state_send,
    state_recv,
    head_sem,
    res_send,
    res_recv,
    dispatch_send,
    dispatch_recv,
    return_send,
    return_recv,
    ag_send,
    ag_recv,
    rs_send,
    rs_recv,
):
    length = query_ref.shape[0]
    width = query_ref.shape[1]
    heads = width // HEAD
    tokens = residual_ref.shape[0]
    model = residual_ref.shape[1]
    hid = down_ref.shape[1]
    half = model // 2
    quarter = model // 4
    block = experts * tokens

    ctx = lax.axis_index("ctx")
    exp = lax.axis_index("exp")
    row, col = ctx // RING, lax.rem(ctx, RING)
    spans = RING * RING

    def along_x(step):
        return {"ctx": lax.rem(row + step, RING) * RING + col}

    def along_y(step):
        return {"ctx": row * RING + lax.rem(col + step, RING)}

    def along_ctx(step):
        return {"ctx": lax.rem(ctx + step, spans)}

    def along_exp(step):
        return {"exp": lax.rem(exp + step, experts)}

    def remote(src, dst, send, recv, device):
        return pltpu.make_async_remote_copy(
            src_ref=src,
            dst_ref=dst,
            send_sem=send,
            recv_sem=recv,
            device_id=device,
            device_id_type=MESH,
        )

    def arrive(buffer, sem):
        pltpu.make_async_copy(buffer, buffer, sem).wait()

    barrier = pltpu.get_barrier_semaphore()
    for step in range(1, experts):
        pl.semaphore_signal(barrier, inc=1, device_id=along_exp(step), device_id_type=MESH)
    for step in range(1, spans):
        pl.semaphore_signal(barrier, inc=1, device_id=along_ctx(step), device_id_type=MESH)

    inputs = [
        pltpu.make_async_copy(source, target, input_sem.at[i])
        for i, (source, target) in enumerate(
            (
                (decay_hbm, decay_ref),
                (key_hbm, key_ref),
                (value_hbm, value_ref),
                (query_hbm, query_ref),
                (ids_hbm, ids_ref),
                (route_hbm, route_ref),
                (residual_hbm, residual_ref),
                (attn_gain_hbm, attn_gain_ref),
                (moe_gain_hbm, moe_gain_ref),
            )
        )
    ]
    weights = [
        pltpu.make_async_copy(gate_ref, gu_weight.at[0:hid], weight_sem.at[0]),
        pltpu.make_async_copy(up_ref, gu_weight.at[hid : 2 * hid], weight_sem.at[1]),
        pltpu.make_async_copy(down_ref.at[0], down_weight, weight_sem.at[2]),
    ]
    for copy in inputs + weights:
        copy.start()
    for copy in inputs:
        copy.wait()

    r = iota((length, length), 0)
    c = iota((length, length), 1)
    causal = r >= c
    decay = decay_ref[...]
    cum = dot(one(causal), decay, ((1,), (1,)), HIGHEST)
    cum_t = dot(decay, one(r <= c), precision=HIGHEST)
    for h in range(heads):
        lanes = slice(h * HEAD, (h + 1) * HEAD)
        total = cum_t[h : h + 1, length - 1 : length]
        scaled = key_ref[:, lanes].astype(F32) * jnp.exp(total - cum[:, h : h + 1])
        update = dot(scaled.astype(BF16), value_ref[:, lanes], ((0,), (0,)))
        state_buf[0, h] = update.astype(BF16)
    total_rows = jnp.where(
        iota((8, HEAD), 0) == 0,
        cum_t[0:1, length - 1 : length],
        cum_t[1:2, length - 1 : length],
    )
    total_buf[pl.ds(ctx, 1)] = total_rows.reshape(1, 8, HEAD)
    for h in range(heads):
        lanes = slice(h * HEAD, (h + 1) * HEAD)
        spread = cum[:, h : h + 1] - cum_t[h : h + 1, :]
        mask = jnp.exp(jnp.where(causal, spread, -jnp.inf))
        scores = dot(query_ref[:, lanes], key_ref[:, lanes], ((1,), (1,)))
        within[:, lanes] = dot((scores * mask).astype(BF16), value_ref[:, lanes])

    lane_s, lane_e = iota((HEAD, tokens), 0) // experts, lax.rem(iota((HEAD, tokens), 0), experts)
    ids = ids_ref[...]
    oh0, oh1 = one(lane_e == ids[0:1, :]), one(lane_e == ids[1:2, :])
    strict = one(iota((tokens, tokens), 0) < iota((tokens, tokens), 1)).astype(BF16)
    count0 = dot((oh0 + oh1).astype(BF16), strict)
    count1 = count0 + oh0
    slot = lane_s.astype(F32)
    take0, take1 = oh0 * one(count0 == slot), oh1 * one(count1 == slot)
    eye = one(iota((tokens, tokens), 0) == iota((tokens, tokens), 1)).astype(BF16)
    own_taken = dot(eye, (take0 + take1).astype(BF16), ((1,), (1,))).astype(BF16)
    taken[pl.ds(exp, 1)] = own_taken.reshape(1, tokens, HEAD)

    block_r, block_c = iota((block, block), 0), iota((block, block), 1)
    high_r, low_r = block_r // tokens, lax.rem(block_r, tokens)
    high_c, low_c = block_c // tokens, lax.rem(block_c, tokens)
    turn = one(jnp.logical_and(high_r == low_c, low_r == high_c)).astype(BF16)
    by_low = one(lax.rem(iota((block, tokens), 0), tokens) == iota((block, tokens), 1)).astype(BF16)
    expert_r = lax.rem(iota((block, HEAD), 0) // tokens + exp, experts)
    by_slot = [
        one(iota((block, HEAD), 1) == expert_r + s * experts).astype(BF16) for s in range(SLOTS)
    ]
    weight = route_ref[0:1, :] * take0 + route_ref[1:2, :] * take1
    weight_high = weight.astype(BF16)
    weight_low = (weight - weight_high.astype(F32)).astype(BF16)
    for part, piece in enumerate((weight_high, weight_low)):
        spread_out = dot(by_low, piece, ((1,), (1,))).astype(BF16)
        for s in range(SLOTS):
            placed = dot(spread_out, by_slot[s], ((1,), (1,)))
            comb[s, part] = jnp.where(high_r == low_c, placed, 0.0).astype(BF16)
    residual_rows = jnp.concatenate(
        [residual_ref[:, j * width : (j + 1) * width] for j in range(experts)], axis=0
    )
    for s in range(SLOTS):
        chosen = dot(by_slot[s], own_taken, ((1,), (1,))).astype(BF16)
        chosen = dot(chosen, by_low, ((1,), (1,)))
        chosen = jnp.where(low_r == high_c, chosen, 0.0).astype(BF16)
        packed_res[s] = dot(chosen, residual_rows).astype(BF16).reshape(experts, tokens, width)

    pl.semaphore_wait(barrier, experts - 1 + spans - 1)

    total_mine = total_buf.at[ctx]
    for step in range(1, spans):
        remote(total_mine, total_mine, total_sem.at[0], total_sem.at[1], along_ctx(step)).start()
    stages = []

    def exchange(source, target, first):
        copies = []
        for step in (1, 3, 2):
            for h in range(heads):
                k = 3 * h + step - 1 + (0 if first else 3 * heads)
                on_y = (h % 2 == 0) == first
                to = along_y(step) if on_y else along_x(step)
                copies.append(
                    remote(
                        source(h, step), target(h, RING - step), state_send.at[k],
                        state_recv.at[k], to,
                    )
                )
        for copy in copies:
            copy.start()
        stages.extend(copies)
        return copies

    stage1 = exchange(lambda h, q: state_buf.at[0, h], lambda h, q: state_buf.at[q, h], True)

    taken_mine = taken.at[exp]
    for step in range(1, experts):
        remote(taken_mine, taken_mine, taken_sem.at[0], taken_sem.at[1], along_exp(step)).start()

    def cross(source, target, send, recv):
        for step in range(1, experts):
            remote(
                source.at[step], target.at[experts - step], send, recv, along_exp(step)
            ).start()
        pltpu.make_async_copy(source.at[0], target.at[0], recv).start()

    for s in range(SLOTS):
        cross(packed_res.at[s], arrived_res.at[s], res_send.at[s], res_recv.at[s])

    others = total_buf.at[1:]
    arrive(others, total_sem.at[1])
    rows4 = RING * RING
    rho = iota((heads * rows4, spans * 8), 0)
    span_m, head_m = iota((heads * rows4, spans * 8), 1) // 8, lax.rem(
        iota((heads * rows4, spans * 8), 1), 8
    )

    def spans_of(index):
        h = index // rows4
        target, source = lax.rem(index, rows4) // RING, lax.rem(index, RING)
        x_t, y_t = lax.rem(row + target, RING) * RING + col, row * RING + lax.rem(col + target, RING)
        x_s, y_s = lax.rem(row + source, RING) * RING + col, row * RING + lax.rem(col + source, RING)
        return h, jnp.where(h == 0, x_t, y_t), jnp.where(h == 0, y_s, x_s)

    h_r, to_r, from_r = spans_of(rho)
    between = jnp.logical_and(jnp.logical_and(from_r < span_m, span_m < to_r), head_m == h_r)
    log_weight = dot(one(between), total_buf[...].reshape(spans * 8, HEAD), precision=HIGHEST)
    _, to_w, from_w = spans_of(iota((heads * rows4, HEAD), 0))
    span_weight = jnp.where(from_w < to_w, jnp.exp(log_weight), 0.0)

    for copy in stage1:
        copy.wait_recv()
    incoming = []
    for h in range(heads):
        states = [state_buf[q, h].astype(F32) for q in range(RING)]
        for target in (1, 3, 2, 0):
            at = h * rows4 + target * RING
            value = span_weight[at : at + 1, :] * states[0]
            for q in range(1, RING):
                value = value + span_weight[at + q : at + q + 1, :] * states[q]
            if target == 0:
                incoming.append(value)
            else:
                message[target, h] = value.astype(BF16)
    stage2 = exchange(lambda h, q: message.at[q, h], lambda h, q: message_in.at[q, h], False)

    others = taken.at[1:]
    arrive(others, taken_sem.at[1])
    all_taken = taken[...].reshape(block, HEAD)
    owner_r = lax.rem(high_r + low_r + exp, experts)
    picks = []
    for s in range(SLOTS):
        chosen = dot(by_slot[s], all_taken, ((1,), (1,)))
        picks.append(jnp.where(owner_r == high_c, chosen, 0.0).astype(BF16))
    for s in range(SLOTS):
        arrive(arrived_res.at[s], res_recv.at[s])

    for copy in stage2:
        copy.wait_recv()

    for h in range(heads):
        lanes = slice(h * HEAD, (h + 1) * HEAD)
        state = incoming[h]
        for q in range(1, RING):
            state = state + message_in[q, h].astype(F32)
        carried = dot(query_ref[:, lanes], state.astype(BF16))
        raw = jnp.exp(cum[:, h : h + 1]) * carried + within[:, lanes]
        scale = lax.rsqrt(jnp.mean(raw * raw, axis=-1, keepdims=True) + EPSILON)
        head_out[:, lanes] = (raw * scale * attn_gain_ref[:, lanes]).astype(BF16)

    for s in range(SLOTS):
        packed[s] = dot(picks[s], head_out[...]).astype(BF16).reshape(experts, tokens, width)
        for step in range(1, experts):
            remote(
                packed.at[s, step], arrived.at[s, exp], dispatch_send.at[s], dispatch_recv.at[s],
                along_exp(step),
            ).start()
        pltpu.make_async_copy(packed.at[s, 0], arrived.at[s, exp], dispatch_recv.at[s]).start()

    def token_rows(device):
        return head_out.at[pl.ds(pl.multiple_of(device * tokens, tokens), tokens), :]

    for step in range(1, experts):
        to = along_exp(step)
        remote(
            token_rows(to["exp"]), head_recv.at[exp], head_sem.at[0], head_sem.at[1], to
        ).start()
    pltpu.make_async_copy(token_rows(exp), head_recv.at[exp], head_sem.at[1]).start()

    def take_rows(s):
        turned = dot(turn, arrived_res[s].reshape(block, width))
        arrive(arrived.at[s], dispatch_recv.at[s])
        squares = jnp.zeros((tokens, 1), F32)
        rows = []
        for j in range(experts):
            value = turned[j * tokens : (j + 1) * tokens, :] + arrived[s, j].astype(F32)
            rows.append(value)
            squares = squares + jnp.sum(value * value, axis=-1, keepdims=True)
        scale = lax.rsqrt(squares / model + EPSILON)
        for j in range(experts):
            lanes = slice(j * width, (j + 1) * width)
            gathered[s, 0, 0, :, lanes] = (rows[j] * scale * moe_gain_ref[:, lanes]).astype(BF16)

    def columns(n, part=None):
        if part is None:
            return slice(n * half, (n + 1) * half)
        start = n * half + part * quarter
        return slice(start, start + quarter)

    def gather_ring(s, phase, n):
        on_x = (phase == 0) == (n == 0)
        step_by = along_x if on_x else along_y

        def view(part, slot):
            if phase == 0:
                at = (slot, 0) if on_x else (0, slot)
                return gathered.at[s, at[0], at[1], :, columns(n, part)]
            two = slice(2 * part, 2 * part + 2)
            if on_x:
                return gathered.at[s, slot, two, :, columns(n)]
            return gathered.at[s, two, slot, :, columns(n)]

        k = (s * 2 + phase) * 2 + n

        if phase == 0 and s in DIRECT_GATHER:
            return [
                remote(
                    view(None, 0), view(None, RING - step), ag_send.at[k, step],
                    ag_recv.at[k, step], step_by(step),
                )
                for step in (1, 3, 2)
            ]

        def make(i, part, source, target, step):
            return remote(
                view(part, source), view(part, target), ag_send.at[k, i], ag_recv.at[k, i],
                step_by(step),
            )

        return [
            make(0, 0, 0, 3, 1),
            make(1, 1, 0, 1, 3),
            make(2, 1, 0, 3, 1),
            make(3, 0, 0, 1, 3),
            make(4, 0, 3, 2, 1),
            make(5, 1, 1, 2, 3),
        ]

    gathers = {
        (s, phase): [gather_ring(s, phase, n) for n in range(2)]
        for s in range(SLOTS)
        for phase in range(2)
    }

    def gather_start(s, phase):
        for i in range(4):
            for ring in gathers[s, phase]:
                if i < len(ring):
                    ring[i].start()

    def gather_forward(s, phase):
        if len(gathers[s, phase][0]) < 6:
            return
        for i in range(2):
            for ring in gathers[s, phase]:
                ring[i].wait_recv()
                ring[4 + i].start()

    def gather_finish(s, phase):
        for ring in gathers[s, phase]:
            for copy in ring[2:] if len(ring) == 6 else ring:
                copy.wait_recv()

    def sum_ring(s, phase, n):
        on_x = (phase == 0) == (n == 1)
        step_by = along_x if on_x else along_y

        def own_view(part, slot):
            if phase == 0:
                two = slice(2 * part, 2 * part + 2)
                if on_x:
                    return partial.at[s, slot, two, :, columns(n)]
                return partial.at[s, two, slot, :, columns(n)]
            at = (slot, 0) if on_x else (0, slot)
            return partial.at[s, at[0], at[1], :, columns(n, part)]

        def opposite(part):
            if phase == 0:
                return opp1.at[s, n, part]
            return opp2.at[s, n, part]

        def final(side, part):
            if phase == 0:
                return fin1.at[s, n, side, 2 * part : 2 * part + 2]
            return fin2.at[s, n, side, :, part * quarter : (part + 1) * quarter]

        k = (s * 2 + phase) * 2 + n

        if phase == 1 and s in DIRECT_SUM:
            copies = [
                remote(
                    own_view(None, step), fin_direct.at[n, RING - step], rs_send.at[k, step],
                    rs_recv.at[k, step], step_by(step),
                )
                for step in (2, 1, 3)
            ]
            return copies, own_view, opposite, final

        def make(i, source, target, step):
            return remote(source, target, rs_send.at[k, i], rs_recv.at[k, i], step_by(step))

        copies = [
            make(0, own_view(0, 2), opposite(0), 1),
            make(1, own_view(1, 2), opposite(1), 3),
            make(2, own_view(1, 1), final(0, 1), 1),
            make(3, own_view(0, 3), final(1, 0), 3),
            make(4, own_view(0, 1), final(0, 0), 1),
            make(5, own_view(1, 3), final(1, 1), 3),
        ]
        return copies, own_view, opposite, final

    sums = {
        (s, phase): [sum_ring(s, phase, n) for n in range(2)]
        for s in range(SLOTS)
        for phase in range(2)
    }

    def sum_start(s, phase):
        for i in range(4):
            for copies, _, _, _ in sums[s, phase]:
                if i < len(copies):
                    copies[i].start()

    def sum_forward(s, phase):
        if len(sums[s, phase][0][0]) < 6:
            return
        for part, slot in ((0, 1), (1, 3)):
            for copies, own_view, opposite, _ in sums[s, phase]:
                copies[part].wait_recv()
                mine = own_view(part, slot)
                mine[...] = (mine[...].astype(F32) + opposite(part)[...].astype(F32)).astype(BF16)
                copies[4 + part].start()

    def sum_finish(s, phase):
        for n, (copies, own_view, _, final) in enumerate(sums[s, phase]):
            if len(copies) < 6:
                for copy in copies:
                    copy.wait_recv()
                mine = own_view(None, 0)
                value = mine[...].astype(F32)
                for q in range(1, RING):
                    value = value + fin_direct[n, q].astype(F32)
                mine[...] = value.astype(BF16)
                continue
            for i in range(2, 6):
                copies[i].wait_recv()
            for part in range(2):
                mine = own_view(part, 0)
                mine[...] = (
                    mine[...].astype(F32)
                    + final(0, part)[...].astype(F32)
                    + final(1, part)[...].astype(F32)
                ).astype(BF16)

    def give_back(s):
        rows = jnp.concatenate(
            [partial[s, 0, 0, :, j * width : (j + 1) * width] for j in range(experts)], axis=0
        )
        back[s] = dot(turn, rows).astype(BF16).reshape(experts, tokens, width)
        cross(back.at[s], returned.at[s], return_send.at[s], return_recv.at[s])

    many = RING * RING * tokens

    def expert_in(s):
        rows = gathered[s].reshape(many, model)
        both = dot(gu_weight[...], rows, ((1,), (1,)))
        act = jax.nn.silu(both[0:hid]) * both[hid : 2 * hid]
        return act.astype(BF16)

    def expert_out(s, act):
        for piece in range(4):
            lanes = slice(piece * quarter, (piece + 1) * quarter)
            made = dot(act, down_weight[:, lanes], ((0,), (0,)))
            partial[s, :, :, :, lanes] = made.astype(BF16).reshape(RING, RING, tokens, quarter)

    take_rows(0)
    gather_start(0, 0)
    take_rows(1)
    gather_forward(0, 0)
    gather_start(1, 0)
    gather_finish(0, 0)
    gather_start(0, 1)
    take_rows(2)
    gather_forward(1, 0)
    gather_forward(0, 1)
    gather_finish(1, 0)
    gather_start(1, 1)
    gather_start(2, 0)
    gather_finish(0, 1)
    for copy in weights:
        copy.wait()
    act = expert_in(0)
    gather_forward(1, 1)
    gather_forward(2, 0)
    gather_finish(2, 0)
    gather_start(2, 1)
    expert_out(0, act)
    sum_start(0, 0)
    gather_finish(1, 1)
    act = expert_in(1)
    gather_forward(2, 1)
    sum_forward(0, 0)
    expert_out(1, act)
    sum_start(1, 0)
    gather_finish(2, 1)
    sum_finish(0, 0)
    sum_start(0, 1)
    act = expert_in(2)
    sum_forward(1, 0)
    sum_forward(0, 1)
    expert_out(2, act)
    sum_start(2, 0)
    sum_finish(0, 1)
    give_back(0)
    sum_finish(1, 0)
    sum_start(1, 1)
    sum_forward(2, 0)
    sum_forward(1, 1)
    sum_finish(1, 1)
    give_back(1)
    sum_finish(2, 0)
    sum_start(2, 1)
    sum_forward(2, 1)
    sum_finish(2, 1)
    give_back(2)

    arrive(head_recv, head_sem.at[1])
    for j in range(experts):
        lanes = slice(j * width, (j + 1) * width)
        hidden[j * tokens : (j + 1) * tokens, :] = (
            residual_ref[:, lanes].astype(F32) + head_recv[j].astype(F32)
        )
    for s in range(SLOTS):
        arrive(returned.at[s], return_recv.at[s])
        rows = returned[s].reshape(block, width)
        hidden[...] += dot(comb[s, 0], rows) + dot(comb[s, 1], rows)
    for j in range(experts):
        out_ref[:, j * width : (j + 1) * width] = hidden[
            j * tokens : (j + 1) * tokens, :
        ].astype(BF16)

    for copy in stages:
        copy.wait_send()
    arrive(total_buf.at[1:], total_sem.at[0])
    arrive(taken.at[1:], taken_sem.at[0])
    arrive(head_recv.at[1:], head_sem.at[0])
    for s in range(SLOTS):
        arrive(arrived_res.at[s, 1:], res_send.at[s])
        arrive(arrived.at[s, 1:], dispatch_send.at[s])
        arrive(returned.at[s, 1:], return_send.at[s])
    for rings in gathers.values():
        for ring in rings:
            for copy in ring:
                copy.wait_send()
    for rings in sums.values():
        for ring in rings:
            for copy in ring[0]:
                copy.wait_send()


def body(
    residual_in,
    query_rows,
    key_rows,
    value_rows,
    log_decay,
    attn_gain,
    moe_gain,
    expert_ids,
    route_weight,
    gate_weight,
    up_weight,
    down_weight,
):
    experts = lax.axis_size("exp")
    tokens, model = residual_in.shape
    length, width = query_rows.shape
    heads = width // HEAD
    hid = down_weight.shape[1]
    half, quarter = model // 2, model // 4
    block = experts * tokens
    dma = pltpu.SemaphoreType.DMA
    vmem = pl.BlockSpec(memory_space=pltpu.VMEM)
    hbm = pl.BlockSpec(memory_space=pl.ANY)
    return pl.pallas_call(
        functools.partial(layer_kernel, experts),
        out_shape=jax.ShapeDtypeStruct((tokens, model), BF16),
        in_specs=[hbm] * 12,
        out_specs=vmem,
        scratch_shapes=[
            pltpu.VMEM((tokens, model), BF16),
            pltpu.VMEM((length, width), BF16),
            pltpu.VMEM((length, width), BF16),
            pltpu.VMEM((length, width), BF16),
            pltpu.VMEM((heads, length), F32),
            pltpu.VMEM((1, width), F32),
            pltpu.VMEM((1, model), F32),
            pltpu.VMEM((2, tokens), jnp.int32),
            pltpu.VMEM((2, tokens), F32),
            pltpu.VMEM((RING * RING, 8, HEAD), F32),
            pltpu.VMEM((RING, heads, HEAD, HEAD), BF16),
            pltpu.VMEM((RING, heads, HEAD, HEAD), BF16),
            pltpu.VMEM((RING, heads, HEAD, HEAD), BF16),
            pltpu.VMEM((length, width), F32),
            pltpu.VMEM((length, width), BF16),
            pltpu.VMEM((experts, tokens, width), BF16),
            pltpu.VMEM((block, width), F32),
            pltpu.VMEM((experts, tokens, HEAD), BF16),
            pltpu.VMEM((SLOTS, 2, block, block), BF16),
            pltpu.VMEM((SLOTS, experts, tokens, width), BF16),
            pltpu.VMEM((SLOTS, experts, tokens, width), BF16),
            pltpu.VMEM((SLOTS, experts, tokens, width), BF16),
            pltpu.VMEM((SLOTS, experts, tokens, width), BF16),
            pltpu.VMEM((SLOTS, RING, RING, tokens, model), BF16),
            pltpu.VMEM((SLOTS, RING, RING, tokens, model), BF16),
            pltpu.VMEM((SLOTS, 2, 2, 2, tokens, half), BF16),
            pltpu.VMEM((SLOTS, 2, 2, RING, tokens, half), BF16),
            pltpu.VMEM((SLOTS, 2, 2, tokens, quarter), BF16),
            pltpu.VMEM((SLOTS, 2, 2, tokens, half), BF16),
            pltpu.VMEM((2, RING, tokens, half), BF16),
            pltpu.VMEM((SLOTS, experts, tokens, width), BF16),
            pltpu.VMEM((SLOTS, experts, tokens, width), BF16),
            pltpu.VMEM((2 * hid, model), BF16),
            pltpu.VMEM((hid, model), BF16),
            dma((9,)),
            dma((3,)),
            dma((2,)),
            dma((2,)),
            dma((6 * heads,)),
            dma((6 * heads,)),
            dma((2,)),
            dma((SLOTS,)),
            dma((SLOTS,)),
            dma((SLOTS,)),
            dma((SLOTS,)),
            dma((SLOTS,)),
            dma((SLOTS,)),
            dma((4 * SLOTS, 6)),
            dma((4 * SLOTS, 6)),
            dma((4 * SLOTS, 6)),
            dma((4 * SLOTS, 6)),
        ],
        compiler_params=pltpu.CompilerParams(
            collective_id=0, has_side_effects=True, vmem_limit_bytes=56 * 1024 * 1024
        ),
    )(
        residual_in,
        query_rows,
        key_rows,
        value_rows,
        log_decay.T,
        attn_gain.reshape(1, -1),
        moe_gain.reshape(1, -1),
        expert_ids.T,
        route_weight.T,
        gate_weight[0].T,
        up_weight[0].T,
        down_weight,
    )


def solution(mesh):
    in_specs = (
        P(("ctx", "exp"), None),
        P("ctx", "exp"),
        P("ctx", "exp"),
        P("ctx", "exp"),
        P("ctx", "exp"),
        P("exp"),
        P(),
        P(("ctx", "exp"), None),
        P(("ctx", "exp"), None),
        P("exp", None, "ctx"),
        P("exp", None, "ctx"),
        P("exp", "ctx", None),
    )
    out_specs = P(("ctx", "exp"), None)
    return jax.shard_map(body, mesh=mesh, in_specs=in_specs, out_specs=out_specs, check_vma=False)
```

```python
import functools

import jax
import jax.numpy as jnp
from jax import lax
from jax.experimental import pallas as pl
from jax.experimental.pallas import tpu as pltpu
from jax.sharding import PartitionSpec as P

HEAD = 128
EPSILON = 1e-05
RING = 4
SLOTS = 3
DIRECT_GATHER = (0, 1, 2)
DIRECT_SUM = (0, 1, 2)
EARLY = (0,)
F32 = jnp.float32
BF16 = jnp.bfloat16
HIGHEST = lax.Precision.HIGHEST
MESH = pl.DeviceIdType.MESH


def iota(shape, dim):
    return lax.broadcasted_iota(jnp.int32, shape, dim)


def dot(a, b, dims=((1,), (0,)), precision=None):
    return lax.dot_general(
        a, b, (dims, ((), ())), precision=precision, preferred_element_type=F32
    )


def one(condition):
    return jnp.where(condition, 1.0, 0.0).astype(F32)


def layer_kernel(
    experts,
    residual_hbm,
    query_hbm,
    key_hbm,
    value_hbm,
    decay_hbm,
    attn_gain_hbm,
    moe_gain_hbm,
    ids_hbm,
    route_hbm,
    gate_ref,
    up_ref,
    down_ref,
    out_ref,
    residual_ref,
    query_ref,
    key_ref,
    value_ref,
    decay_ref,
    attn_gain_ref,
    moe_gain_ref,
    ids_ref,
    route_ref,
    total_buf,
    state_buf,
    message,
    message_in,
    within,
    head_out,
    head_recv,
    hidden,
    taken,
    comb,
    packed_res,
    arrived_res,
    packed,
    arrived,
    gathered,
    partial,
    opp1,
    fin1,
    opp2,
    fin2,
    fin_direct,
    back,
    returned,
    gu_weight,
    down_weight,
    input_sem,
    weight_sem,
    total_sem,
    taken_sem,
    state_send,
    state_recv,
    head_sem,
    res_send,
    res_recv,
    dispatch_send,
    dispatch_recv,
    return_send,
    return_recv,
    ag_send,
    ag_recv,
    rs_send,
    rs_recv,
):
    length = query_ref.shape[0]
    width = query_ref.shape[1]
    heads = width // HEAD
    tokens = residual_ref.shape[0]
    model = residual_ref.shape[1]
    hid = down_ref.shape[1]
    half = model // 2
    quarter = model // 4
    block = experts * tokens

    ctx = lax.axis_index("ctx")
    exp = lax.axis_index("exp")
    row, col = ctx // RING, lax.rem(ctx, RING)
    spans = RING * RING

    def along_x(step):
        return {"ctx": lax.rem(row + step, RING) * RING + col}

    def along_y(step):
        return {"ctx": row * RING + lax.rem(col + step, RING)}

    def along_ctx(step):
        return {"ctx": lax.rem(ctx + step, spans)}

    def along_exp(step):
        return {"exp": lax.rem(exp + step, experts)}

    def remote(src, dst, send, recv, device):
        return pltpu.make_async_remote_copy(
            src_ref=src,
            dst_ref=dst,
            send_sem=send,
            recv_sem=recv,
            device_id=device,
            device_id_type=MESH,
        )

    def arrive(buffer, sem):
        pltpu.make_async_copy(buffer, buffer, sem).wait()

    barrier = pltpu.get_barrier_semaphore()
    for step in range(1, experts):
        pl.semaphore_signal(barrier, inc=1, device_id=along_exp(step), device_id_type=MESH)
    for step in range(1, spans):
        pl.semaphore_signal(barrier, inc=1, device_id=along_ctx(step), device_id_type=MESH)

    inputs = [
        pltpu.make_async_copy(source, target, input_sem.at[i])
        for i, (source, target) in enumerate(
            (
                (decay_hbm, decay_ref),
                (key_hbm, key_ref),
                (value_hbm, value_ref),
                (query_hbm, query_ref),
                (ids_hbm, ids_ref),
                (route_hbm, route_ref),
                (residual_hbm, residual_ref),
                (attn_gain_hbm, attn_gain_ref),
                (moe_gain_hbm, moe_gain_ref),
            )
        )
    ]
    weights = [
        pltpu.make_async_copy(gate_ref, gu_weight.at[0:hid], weight_sem.at[0]),
        pltpu.make_async_copy(up_ref, gu_weight.at[hid : 2 * hid], weight_sem.at[1]),
        pltpu.make_async_copy(down_ref.at[0], down_weight, weight_sem.at[2]),
    ]
    for copy in inputs + weights:
        copy.start()
    for copy in inputs:
        copy.wait()

    r = iota((length, length), 0)
    c = iota((length, length), 1)
    causal = r >= c
    decay = decay_ref[...]
    cum = dot(one(causal), decay, ((1,), (1,)), HIGHEST)
    cum_t = dot(decay, one(r <= c), precision=HIGHEST)
    for h in range(heads):
        lanes = slice(h * HEAD, (h + 1) * HEAD)
        total = cum_t[h : h + 1, length - 1 : length]
        scaled = key_ref[:, lanes].astype(F32) * jnp.exp(total - cum[:, h : h + 1])
        update = dot(scaled.astype(BF16), value_ref[:, lanes], ((0,), (0,)))
        state_buf[0, h] = update.astype(BF16)
    total_rows = jnp.where(
        iota((8, HEAD), 0) == 0,
        cum_t[0:1, length - 1 : length],
        cum_t[1:2, length - 1 : length],
    )
    total_buf[pl.ds(ctx, 1)] = total_rows.reshape(1, 8, HEAD)
    for h in range(heads):
        lanes = slice(h * HEAD, (h + 1) * HEAD)
        spread = cum[:, h : h + 1] - cum_t[h : h + 1, :]
        mask = jnp.exp(jnp.where(causal, spread, -jnp.inf))
        scores = dot(query_ref[:, lanes], key_ref[:, lanes], ((1,), (1,)))
        within[:, lanes] = dot((scores * mask).astype(BF16), value_ref[:, lanes])

    lane_s, lane_e = iota((HEAD, tokens), 0) // experts, lax.rem(iota((HEAD, tokens), 0), experts)
    ids = ids_ref[...]
    oh0, oh1 = one(lane_e == ids[0:1, :]), one(lane_e == ids[1:2, :])
    strict = one(iota((tokens, tokens), 0) < iota((tokens, tokens), 1)).astype(BF16)
    count0 = dot((oh0 + oh1).astype(BF16), strict)
    count1 = count0 + oh0
    slot = lane_s.astype(F32)
    take0, take1 = oh0 * one(count0 == slot), oh1 * one(count1 == slot)
    eye = one(iota((tokens, tokens), 0) == iota((tokens, tokens), 1)).astype(BF16)
    own_taken = dot(eye, (take0 + take1).astype(BF16), ((1,), (1,))).astype(BF16)
    taken[pl.ds(exp, 1)] = own_taken.reshape(1, tokens, HEAD)

    block_r, block_c = iota((block, block), 0), iota((block, block), 1)
    high_r, low_r = block_r // tokens, lax.rem(block_r, tokens)
    high_c, low_c = block_c // tokens, lax.rem(block_c, tokens)
    turn = one(jnp.logical_and(high_r == low_c, low_r == high_c)).astype(BF16)
    by_low = one(lax.rem(iota((block, tokens), 0), tokens) == iota((block, tokens), 1)).astype(BF16)
    expert_r = lax.rem(iota((block, HEAD), 0) // tokens + exp, experts)
    by_slot = [
        one(iota((block, HEAD), 1) == expert_r + s * experts).astype(BF16) for s in range(SLOTS)
    ]
    weight = route_ref[0:1, :] * take0 + route_ref[1:2, :] * take1
    weight_high = weight.astype(BF16)
    weight_low = (weight - weight_high.astype(F32)).astype(BF16)
    for part, piece in enumerate((weight_high, weight_low)):
        spread_out = dot(by_low, piece, ((1,), (1,))).astype(BF16)
        for s in range(SLOTS):
            placed = dot(spread_out, by_slot[s], ((1,), (1,)))
            comb[s, part] = jnp.where(high_r == low_c, placed, 0.0).astype(BF16)
    residual_rows = jnp.concatenate(
        [residual_ref[:, j * width : (j + 1) * width] for j in range(experts)], axis=0
    )
    for s in range(SLOTS):
        chosen = dot(by_slot[s], own_taken, ((1,), (1,))).astype(BF16)
        chosen = dot(chosen, by_low, ((1,), (1,)))
        chosen = jnp.where(low_r == high_c, chosen, 0.0).astype(BF16)
        packed_res[s] = dot(chosen, residual_rows).astype(BF16).reshape(experts, tokens, width)

    pl.semaphore_wait(barrier, experts - 1 + spans - 1)

    total_mine = total_buf.at[ctx]
    for step in range(1, spans):
        remote(total_mine, total_mine, total_sem.at[0], total_sem.at[1], along_ctx(step)).start()
    stages = []

    def exchange(source, target, first):
        copies = []
        for step in (1, 3, 2):
            for h in range(heads):
                k = 3 * h + step - 1 + (0 if first else 3 * heads)
                on_y = (h % 2 == 0) == first
                to = along_y(step) if on_y else along_x(step)
                copies.append(
                    remote(
                        source(h, step), target(h, RING - step), state_send.at[k],
                        state_recv.at[k], to,
                    )
                )
        for copy in copies:
            copy.start()
        stages.extend(copies)
        return copies

    stage1 = exchange(lambda h, q: state_buf.at[0, h], lambda h, q: state_buf.at[q, h], True)

    taken_mine = taken.at[exp]
    for step in range(1, experts):
        remote(taken_mine, taken_mine, taken_sem.at[0], taken_sem.at[1], along_exp(step)).start()

    def cross(source, target, send, recv):
        for step in range(1, experts):
            remote(
                source.at[step], target.at[experts - step], send, recv, along_exp(step)
            ).start()
        pltpu.make_async_copy(source.at[0], target.at[0], recv).start()

    def send_residual(s):
        cross(packed_res.at[s], arrived_res.at[s], res_send.at[s], res_recv.at[s])

    send_residual(0)
    send_residual(1)
    send_residual(2)

    others = total_buf.at[1:]
    arrive(others, total_sem.at[1])
    rows4 = RING * RING
    rho = iota((heads * rows4, spans * 8), 0)
    span_m, head_m = iota((heads * rows4, spans * 8), 1) // 8, lax.rem(
        iota((heads * rows4, spans * 8), 1), 8
    )

    def spans_of(index):
        h = index // rows4
        target, source = lax.rem(index, rows4) // RING, lax.rem(index, RING)
        x_t, y_t = lax.rem(row + target, RING) * RING + col, row * RING + lax.rem(col + target, RING)
        x_s, y_s = lax.rem(row + source, RING) * RING + col, row * RING + lax.rem(col + source, RING)
        return h, jnp.where(h == 0, x_t, y_t), jnp.where(h == 0, y_s, x_s)

    h_r, to_r, from_r = spans_of(rho)
    between = jnp.logical_and(jnp.logical_and(from_r < span_m, span_m < to_r), head_m == h_r)
    log_weight = dot(one(between), total_buf[...].reshape(spans * 8, HEAD), precision=HIGHEST)
    _, to_w, from_w = spans_of(iota((heads * rows4, HEAD), 0))
    span_weight = jnp.where(from_w < to_w, jnp.exp(log_weight), 0.0)

    for copy in stage1:
        copy.wait_recv()
    incoming = []
    for h in range(heads):
        states = [state_buf[q, h].astype(F32) for q in range(RING)]
        for target in (1, 3, 2, 0):
            at = h * rows4 + target * RING
            value = span_weight[at : at + 1, :] * states[0]
            for q in range(1, RING):
                value = value + span_weight[at + q : at + q + 1, :] * states[q]
            if target == 0:
                incoming.append(value)
            else:
                message[target, h] = value.astype(BF16)
    stage2 = exchange(lambda h, q: message.at[q, h], lambda h, q: message_in.at[q, h], False)

    others = taken.at[1:]
    arrive(others, taken_sem.at[1])
    all_taken = taken[...].reshape(block, HEAD)
    owner_r = lax.rem(high_r + low_r + exp, experts)
    picks = []
    for s in range(SLOTS):
        chosen = dot(by_slot[s], all_taken, ((1,), (1,)))
        picks.append(jnp.where(owner_r == high_c, chosen, 0.0).astype(BF16))

    for copy in stage2:
        copy.wait_recv()

    for h in range(heads):
        lanes = slice(h * HEAD, (h + 1) * HEAD)
        state = incoming[h]
        for q in range(1, RING):
            state = state + message_in[q, h].astype(F32)
        carried = dot(query_ref[:, lanes], state.astype(BF16))
        raw = jnp.exp(cum[:, h : h + 1]) * carried + within[:, lanes]
        scale = lax.rsqrt(jnp.mean(raw * raw, axis=-1, keepdims=True) + EPSILON)
        head_out[:, lanes] = (raw * scale * attn_gain_ref[:, lanes]).astype(BF16)

    def send_columns(s):
        packed[s] = dot(picks[s], head_out[...]).astype(BF16).reshape(experts, tokens, width)
        for step in range(1, experts):
            remote(
                packed.at[s, step], arrived.at[s, exp], dispatch_send.at[s], dispatch_recv.at[s],
                along_exp(step),
            ).start()
        pltpu.make_async_copy(packed.at[s, 0], arrived.at[s, exp], dispatch_recv.at[s]).start()

    def token_rows(device):
        return head_out.at[pl.ds(pl.multiple_of(device * tokens, tokens), tokens), :]

    def send_owners():
        for step in range(1, experts):
            to = along_exp(step)
            remote(
                token_rows(to["exp"]), head_recv.at[exp], head_sem.at[0], head_sem.at[1], to
            ).start()
        pltpu.make_async_copy(token_rows(exp), head_recv.at[exp], head_sem.at[1]).start()

    def take_rows(s):
        arrive(arrived_res.at[s], res_recv.at[s])
        turned = dot(turn, arrived_res[s].reshape(block, width))
        arrive(arrived.at[s], dispatch_recv.at[s])
        squares = jnp.zeros((tokens, width), F32)
        rows = []
        for j in range(experts):
            value = turned[j * tokens : (j + 1) * tokens, :] + arrived[s, j].astype(F32)
            rows.append(value)
            squares = squares + value * value
        scale = lax.rsqrt(jnp.sum(squares, axis=-1, keepdims=True) / model + EPSILON)
        for j in range(experts):
            lanes = slice(j * width, (j + 1) * width)
            gathered[s, 0, 0, :, lanes] = (rows[j] * scale * moe_gain_ref[:, lanes]).astype(BF16)

    def columns(n, part=None):
        if part is None:
            return slice(n * half, (n + 1) * half)
        start = n * half + part * quarter
        return slice(start, start + quarter)

    def gather_ring(s, phase, n):
        on_x = (phase == 0) == (n == 0)
        step_by = along_x if on_x else along_y

        def view(part, slot):
            if phase == 0:
                at = (slot, 0) if on_x else (0, slot)
                return gathered.at[s, at[0], at[1], :, columns(n, part)]
            return blocks_view(slice(2 * part, 2 * part + 2), slot)

        def blocks_view(blocks, slot):
            if on_x:
                return gathered.at[s, slot, blocks, :, columns(n)]
            return gathered.at[s, blocks, slot, :, columns(n)]

        k = (s * 2 + phase) * 2 + n

        if phase == 0 and s in DIRECT_GATHER:
            return [
                remote(
                    view(None, 0), view(None, RING - step), ag_send.at[k, step],
                    ag_recv.at[k, step], step_by(step),
                )
                for step in (1, 3, 2)
            ]

        def make(i, part, source, target, step):
            return remote(
                view(part, source), view(part, target), ag_send.at[k, i], ag_recv.at[k, i],
                step_by(step),
            )

        def make_block(i, block, target, step):
            return remote(
                blocks_view(block, 0), blocks_view(block, target), ag_send.at[k, i],
                ag_recv.at[k, i], step_by(step),
            )

        early = phase == 1 and s in EARLY
        return [
            make_block(0, 1, 3, 1) if early else make(0, 0, 0, 3, 1),
            make(1, 1, 0, 1, 3),
            make(2, 1, 0, 3, 1),
            make_block(3, 1, 1, 3) if early else make(3, 0, 0, 1, 3),
            make(4, 0, 3, 2, 1),
            make(5, 1, 1, 2, 3),
        ] + ([make_block(6, 0, 3, 1), make_block(7, 0, 1, 3)] if early else [])

    gathers = {
        (s, phase): [gather_ring(s, phase, n) for n in range(2)]
        for s in range(SLOTS)
        for phase in range(2)
    }

    def gather_early(s):
        for i in (6, 7):
            for ring in gathers[s, 1]:
                ring[i].start()

    def gather_start(s, phase):
        for i in range(4):
            for ring in gathers[s, phase]:
                if i < len(ring):
                    ring[i].start()

    def gather_forward(s, phase):
        if len(gathers[s, phase][0]) < 6:
            return
        for i in range(2):
            for ring in gathers[s, phase]:
                ring[i].wait_recv()
                if i == 0 and len(ring) > 6:
                    ring[6].wait_recv()
                ring[4 + i].start()

    def gather_finish(s, phase):
        for ring in gathers[s, phase]:
            for copy in ring if len(ring) < 6 else ring[2:6] + ring[7:]:
                copy.wait_recv()

    def sum_ring(s, phase, n):
        on_x = (phase == 0) == (n == 1)
        step_by = along_x if on_x else along_y

        def own_view(part, slot):
            if phase == 0:
                two = slice(2 * part, 2 * part + 2)
                if on_x:
                    return partial.at[s, slot, two, :, columns(n)]
                return partial.at[s, two, slot, :, columns(n)]
            at = (slot, 0) if on_x else (0, slot)
            return partial.at[s, at[0], at[1], :, columns(n, part)]

        def opposite(part):
            if phase == 0:
                return opp1.at[s, n, part]
            return opp2.at[s, n, part]

        def final(side, part):
            if phase == 0:
                return fin1.at[s, n, side, 2 * part : 2 * part + 2]
            return fin2.at[s, n, side, :, part * quarter : (part + 1) * quarter]

        k = (s * 2 + phase) * 2 + n

        if phase == 1 and s in DIRECT_SUM:
            copies = [
                remote(
                    own_view(None, step), fin_direct.at[s, n, RING - step], rs_send.at[k, step],
                    rs_recv.at[k, step], step_by(step),
                )
                for step in (2, 1, 3)
            ]
            return copies, own_view, opposite, final

        def make(i, source, target, step):
            return remote(source, target, rs_send.at[k, i], rs_recv.at[k, i], step_by(step))

        copies = [
            make(0, own_view(0, 2), opposite(0), 1),
            make(1, own_view(1, 2), opposite(1), 3),
            make(2, own_view(1, 1), final(0, 1), 1),
            make(3, own_view(0, 3), final(1, 0), 3),
            make(4, own_view(0, 1), final(0, 0), 1),
            make(5, own_view(1, 3), final(1, 1), 3),
        ]
        return copies, own_view, opposite, final

    sums = {
        (s, phase): [sum_ring(s, phase, n) for n in range(2)]
        for s in range(SLOTS)
        for phase in range(2)
    }

    def sum_start(s, phase):
        for i in range(4):
            for copies, _, _, _ in sums[s, phase]:
                if i < len(copies):
                    copies[i].start()

    def sum_forward(s, phase):
        if len(sums[s, phase][0][0]) < 6:
            return
        for part, slot in ((0, 1), (1, 3)):
            for copies, own_view, opposite, _ in sums[s, phase]:
                copies[part].wait_recv()
                mine = own_view(part, slot)
                mine[...] = (mine[...].astype(F32) + opposite(part)[...].astype(F32)).astype(BF16)
                copies[4 + part].start()

    def sum_finish(s, phase):
        for n, (copies, own_view, _, final) in enumerate(sums[s, phase]):
            if len(copies) < 6:
                for copy in copies:
                    copy.wait_recv()
                mine = own_view(None, 0)
                value = mine[...].astype(F32)
                for q in range(1, RING):
                    value = value + fin_direct[s, n, q].astype(F32)
                mine[...] = value.astype(BF16)
                continue
            for i in range(2, 6):
                copies[i].wait_recv()
            for part in range(2):
                mine = own_view(part, 0)
                mine[...] = (
                    mine[...].astype(F32)
                    + final(0, part)[...].astype(F32)
                    + final(1, part)[...].astype(F32)
                ).astype(BF16)

    def give_back(s):
        rows = jnp.concatenate(
            [partial[s, 0, 0, :, j * width : (j + 1) * width] for j in range(experts)], axis=0
        )
        back[s] = dot(turn, rows).astype(BF16).reshape(experts, tokens, width)
        cross(back.at[s], returned.at[s], return_send.at[s], return_recv.at[s])

    many = RING * RING * tokens

    def expert_gate(s):
        return dot(gu_weight[0:hid], gathered[s].reshape(many, model), ((1,), (1,)))

    def expert_up(s, gate):
        up = dot(gu_weight[hid : 2 * hid], gathered[s].reshape(many, model), ((1,), (1,)))
        return (jax.nn.silu(gate) * up).astype(BF16)

    def expert_out(s, act):
        for n in range(2):
            for piece in (2 * n, 2 * n + 1):
                lanes = slice(piece * quarter, (piece + 1) * quarter)
                made = dot(act, down_weight[:, lanes], ((0,), (0,)))
                partial[s, :, :, :, lanes] = made.astype(BF16).reshape(
                    RING, RING, tokens, quarter
                )
            for i in range(4):
                sums[s, 0][n][0][i].start()

    send_columns(0)
    send_columns(1)
    send_columns(2)

    def own_rows():
        arrive(head_recv, head_sem.at[1])
        for j in range(experts):
            lanes = slice(j * width, (j + 1) * width)
            hidden[j * tokens : (j + 1) * tokens, :] = (
                residual_ref[:, lanes].astype(F32) + head_recv[j].astype(F32)
            )

    def combine(s):
        arrive(returned.at[s], return_recv.at[s])
        rows = returned[s].reshape(block, width)
        hidden[...] += dot(comb[s, 0], rows) + dot(comb[s, 1], rows)

    def gathers_left(s):
        for phase in range(2):
            for ring in gathers[s, phase]:
                for copy in ring:
                    copy.wait_send()
        arrive(arrived_res.at[s, 1:], res_send.at[s])
        arrive(arrived.at[s, 1:], dispatch_send.at[s])

    def sums_left(s, phase):
        for ring in sums[s, phase]:
            for copy in ring[0]:
                copy.wait_send()

    def first_left():
        for copy in stages:
            copy.wait_send()
        arrive(total_buf.at[1:], total_sem.at[0])
        arrive(taken.at[1:], taken_sem.at[0])
        arrive(head_recv.at[1:], head_sem.at[0])

    take_rows(0)
    gather_start(0, 0)
    gather_early(0)
    send_owners()
    gather_finish(0, 0)
    gather_start(0, 1)
    take_rows(1)
    gather_start(1, 0)
    take_rows(2)
    gather_forward(1, 0)
    gather_forward(0, 1)
    gather_finish(1, 0)
    gather_start(1, 1)
    gather_start(2, 0)
    gather_finish(0, 1)
    for copy in weights:
        copy.wait()
    gate = expert_gate(0)
    gather_forward(1, 1)
    act = expert_up(0, gate)
    gather_forward(2, 0)
    gather_finish(2, 0)
    gather_start(2, 1)
    expert_out(0, act)
    gather_finish(1, 1)
    gate = expert_gate(1)
    gather_forward(2, 1)
    act = expert_up(1, gate)
    sum_forward(0, 0)
    expert_out(1, act)
    gather_finish(2, 1)
    sum_finish(0, 0)
    sum_start(0, 1)
    gate = expert_gate(2)
    sum_forward(1, 0)
    act = expert_up(2, gate)
    sum_forward(0, 1)
    expert_out(2, act)
    sum_finish(0, 1)
    give_back(0)
    first_left()
    own_rows()
    sum_finish(1, 0)
    sum_start(1, 1)
    sum_forward(2, 0)
    sum_forward(1, 1)
    sum_finish(1, 1)
    give_back(1)
    for s in range(SLOTS):
        gathers_left(s)
    combine(0)
    sum_finish(2, 0)
    sum_start(2, 1)
    for s in range(SLOTS - 1):
        sums_left(s, 0)
        sums_left(s, 1)
    arrive(returned.at[0, 1:], return_send.at[0])
    sum_finish(2, 1)
    give_back(2)
    combine(1)
    arrive(returned.at[1, 1:], return_send.at[1])
    sums_left(2, 0)
    sums_left(2, 1)

    combine(2)
    for j in range(experts):
        out_ref[:, j * width : (j + 1) * width] = hidden[
            j * tokens : (j + 1) * tokens, :
        ].astype(BF16)
    arrive(returned.at[2, 1:], return_send.at[2])


def body(
    residual_in,
    query_rows,
    key_rows,
    value_rows,
    log_decay,
    attn_gain,
    moe_gain,
    expert_ids,
    route_weight,
    gate_weight,
    up_weight,
    down_weight,
):
    experts = lax.axis_size("exp")
    tokens, model = residual_in.shape
    length, width = query_rows.shape
    heads = width // HEAD
    hid = down_weight.shape[1]
    half, quarter = model // 2, model // 4
    block = experts * tokens
    dma = pltpu.SemaphoreType.DMA
    vmem = pl.BlockSpec(memory_space=pltpu.VMEM)
    hbm = pl.BlockSpec(memory_space=pl.ANY)
    return pl.pallas_call(
        functools.partial(layer_kernel, experts),
        out_shape=jax.ShapeDtypeStruct((tokens, model), BF16),
        in_specs=[hbm] * 12,
        out_specs=vmem,
        scratch_shapes=[
            pltpu.VMEM((tokens, model), BF16),
            pltpu.VMEM((length, width), BF16),
            pltpu.VMEM((length, width), BF16),
            pltpu.VMEM((length, width), BF16),
            pltpu.VMEM((heads, length), F32),
            pltpu.VMEM((1, width), F32),
            pltpu.VMEM((1, model), F32),
            pltpu.VMEM((2, tokens), jnp.int32),
            pltpu.VMEM((2, tokens), F32),
            pltpu.VMEM((RING * RING, 8, HEAD), F32),
            pltpu.VMEM((RING, heads, HEAD, HEAD), BF16),
            pltpu.VMEM((RING, heads, HEAD, HEAD), BF16),
            pltpu.VMEM((RING, heads, HEAD, HEAD), BF16),
            pltpu.VMEM((length, width), F32),
            pltpu.VMEM((length, width), BF16),
            pltpu.VMEM((experts, tokens, width), BF16),
            pltpu.VMEM((block, width), F32),
            pltpu.VMEM((experts, tokens, HEAD), BF16),
            pltpu.VMEM((SLOTS, 2, block, block), BF16),
            pltpu.VMEM((SLOTS, experts, tokens, width), BF16),
            pltpu.VMEM((SLOTS, experts, tokens, width), BF16),
            pltpu.VMEM((SLOTS, experts, tokens, width), BF16),
            pltpu.VMEM((SLOTS, experts, tokens, width), BF16),
            pltpu.VMEM((SLOTS, RING, RING, tokens, model), BF16),
            pltpu.VMEM((SLOTS, RING, RING, tokens, model), BF16),
            pltpu.VMEM((SLOTS, 2, 2, 2, tokens, half), BF16),
            pltpu.VMEM((SLOTS, 2, 2, RING, tokens, half), BF16),
            pltpu.VMEM((SLOTS, 2, 2, tokens, quarter), BF16),
            pltpu.VMEM((SLOTS, 2, 2, tokens, half), BF16),
            pltpu.VMEM((SLOTS, 2, RING, tokens, half), BF16),
            pltpu.VMEM((SLOTS, experts, tokens, width), BF16),
            pltpu.VMEM((SLOTS, experts, tokens, width), BF16),
            pltpu.VMEM((2 * hid, model), BF16),
            pltpu.VMEM((hid, model), BF16),
            dma((9,)),
            dma((3,)),
            dma((2,)),
            dma((2,)),
            dma((6 * heads,)),
            dma((6 * heads,)),
            dma((2,)),
            dma((SLOTS,)),
            dma((SLOTS,)),
            dma((SLOTS,)),
            dma((SLOTS,)),
            dma((SLOTS,)),
            dma((SLOTS,)),
            dma((4 * SLOTS, 8)),
            dma((4 * SLOTS, 8)),
            dma((4 * SLOTS, 6)),
            dma((4 * SLOTS, 6)),
        ],
        compiler_params=pltpu.CompilerParams(
            collective_id=0, has_side_effects=True, vmem_limit_bytes=56 * 1024 * 1024
        ),
    )(
        residual_in,
        query_rows,
        key_rows,
        value_rows,
        log_decay.T,
        attn_gain.reshape(1, -1),
        moe_gain.reshape(1, -1),
        expert_ids.T,
        route_weight.T,
        gate_weight[0].T,
        up_weight[0].T,
        down_weight,
    )


def solution(mesh):
    in_specs = (
        P(("ctx", "exp"), None),
        P("ctx", "exp"),
        P("ctx", "exp"),
        P("ctx", "exp"),
        P("ctx", "exp"),
        P("exp"),
        P(),
        P(("ctx", "exp"), None),
        P(("ctx", "exp"), None),
        P("exp", None, "ctx"),
        P("exp", None, "ctx"),
        P("exp", "ctx", None),
    )
    out_specs = P(("ctx", "exp"), None)
    return jax.shard_map(body, mesh=mesh, in_specs=in_specs, out_specs=out_specs, check_vma=False)
```

```python
import functools

import jax
import jax.numpy as jnp
from jax import lax
from jax.experimental import pallas as pl
from jax.experimental.pallas import tpu as pltpu
from jax.sharding import PartitionSpec as P

HEAD = 128
EPSILON = 1e-05
RING = 4
SLOTS = 3
DIRECT_GATHER = (0, 1, 2)
DIRECT_SUM = (0, 1, 2)
EARLY = (0, 1, 2)
F32 = jnp.float32
BF16 = jnp.bfloat16
HIGHEST = lax.Precision.HIGHEST
MESH = pl.DeviceIdType.MESH


def iota(shape, dim):
    return lax.broadcasted_iota(jnp.int32, shape, dim)


def dot(a, b, dims=((1,), (0,)), precision=None):
    return lax.dot_general(
        a, b, (dims, ((), ())), precision=precision, preferred_element_type=F32
    )


def one(condition):
    return jnp.where(condition, 1.0, 0.0).astype(F32)


def layer_kernel(
    experts,
    residual_hbm,
    query_hbm,
    key_hbm,
    value_hbm,
    decay_hbm,
    attn_gain_hbm,
    moe_gain_hbm,
    ids_hbm,
    route_hbm,
    gate_ref,
    up_ref,
    down_ref,
    out_ref,
    residual_ref,
    query_ref,
    key_ref,
    value_ref,
    decay_ref,
    attn_gain_ref,
    moe_gain_ref,
    ids_ref,
    route_ref,
    total_buf,
    state_buf,
    message,
    message_in,
    within,
    head_out,
    head_recv,
    hidden,
    taken,
    comb,
    packed_res,
    arrived_res,
    packed,
    arrived,
    gathered,
    partial,
    opp1,
    fin1,
    opp2,
    fin2,
    fin_direct,
    back,
    returned,
    gu_weight,
    down_weight,
    input_sem,
    weight_sem,
    total_sem,
    taken_sem,
    state_send,
    state_recv,
    head_sem,
    res_send,
    res_recv,
    dispatch_send,
    dispatch_recv,
    return_send,
    return_recv,
    ag_send,
    ag_recv,
    rs_send,
    rs_recv,
):
    length = query_ref.shape[0]
    width = query_ref.shape[1]
    heads = width // HEAD
    tokens = residual_ref.shape[0]
    model = residual_ref.shape[1]
    hid = down_ref.shape[1]
    half = model // 2
    quarter = model // 4
    block = experts * tokens

    ctx = lax.axis_index("ctx")
    exp = lax.axis_index("exp")
    row, col = ctx // RING, lax.rem(ctx, RING)
    spans = RING * RING

    def along_x(step):
        return {"ctx": lax.rem(row + step, RING) * RING + col}

    def along_y(step):
        return {"ctx": row * RING + lax.rem(col + step, RING)}

    def along_ctx(step):
        return {"ctx": lax.rem(ctx + step, spans)}

    def along_exp(step):
        return {"exp": lax.rem(exp + step, experts)}

    def remote(src, dst, send, recv, device):
        return pltpu.make_async_remote_copy(
            src_ref=src,
            dst_ref=dst,
            send_sem=send,
            recv_sem=recv,
            device_id=device,
            device_id_type=MESH,
        )

    def arrive(buffer, sem):
        pltpu.make_async_copy(buffer, buffer, sem).wait()

    far_first = sorted(range(1, experts), key=lambda step: -min(step, experts - step))

    barrier = pltpu.get_barrier_semaphore()
    for step in range(1, experts):
        pl.semaphore_signal(barrier, inc=1, device_id=along_exp(step), device_id_type=MESH)
    for step in range(1, spans):
        pl.semaphore_signal(barrier, inc=1, device_id=along_ctx(step), device_id_type=MESH)

    inputs = [
        pltpu.make_async_copy(source, target, input_sem.at[i])
        for i, (source, target) in enumerate(
            (
                (decay_hbm, decay_ref),
                (key_hbm, key_ref),
                (value_hbm, value_ref),
                (query_hbm, query_ref),
                (ids_hbm, ids_ref),
                (route_hbm, route_ref),
                (residual_hbm, residual_ref),
                (attn_gain_hbm, attn_gain_ref),
                (moe_gain_hbm, moe_gain_ref),
            )
        )
    ]
    weights = [
        pltpu.make_async_copy(gate_ref, gu_weight.at[0:hid], weight_sem.at[0]),
        pltpu.make_async_copy(up_ref, gu_weight.at[hid : 2 * hid], weight_sem.at[1]),
        pltpu.make_async_copy(down_ref.at[0], down_weight, weight_sem.at[2]),
    ]
    for copy in inputs + weights:
        copy.start()
    for copy in inputs:
        copy.wait()

    r = iota((length, length), 0)
    c = iota((length, length), 1)
    causal = r >= c
    decay = decay_ref[...]
    cum = dot(one(causal), decay, ((1,), (1,)), HIGHEST)
    cum_t = dot(decay, one(r <= c), precision=HIGHEST)
    for h in range(heads):
        lanes = slice(h * HEAD, (h + 1) * HEAD)
        total = cum_t[h : h + 1, length - 1 : length]
        scaled = key_ref[:, lanes].astype(F32) * jnp.exp(total - cum[:, h : h + 1])
        update = dot(scaled.astype(BF16), value_ref[:, lanes], ((0,), (0,)))
        state_buf[0, h] = update.astype(BF16)
    total_rows = jnp.where(
        iota((8, HEAD), 0) == 0,
        cum_t[0:1, length - 1 : length],
        cum_t[1:2, length - 1 : length],
    )
    total_buf[pl.ds(ctx, 1)] = total_rows.reshape(1, 8, HEAD)
    for h in range(heads):
        lanes = slice(h * HEAD, (h + 1) * HEAD)
        spread = cum[:, h : h + 1] - cum_t[h : h + 1, :]
        mask = jnp.exp(jnp.where(causal, spread, -jnp.inf))
        scores = dot(query_ref[:, lanes], key_ref[:, lanes], ((1,), (1,)))
        within[:, lanes] = dot((scores * mask).astype(BF16), value_ref[:, lanes])

    lane_s, lane_e = iota((HEAD, tokens), 0) // experts, lax.rem(iota((HEAD, tokens), 0), experts)
    ids = ids_ref[...]
    oh0, oh1 = one(lane_e == ids[0:1, :]), one(lane_e == ids[1:2, :])
    strict = one(iota((tokens, tokens), 0) < iota((tokens, tokens), 1)).astype(BF16)
    count0 = dot((oh0 + oh1).astype(BF16), strict)
    count1 = count0 + oh0
    slot = lane_s.astype(F32)
    take0, take1 = oh0 * one(count0 == slot), oh1 * one(count1 == slot)
    eye = one(iota((tokens, tokens), 0) == iota((tokens, tokens), 1)).astype(BF16)
    own_taken = dot(eye, (take0 + take1).astype(BF16), ((1,), (1,))).astype(BF16)
    taken[pl.ds(exp, 1)] = own_taken.reshape(1, tokens, HEAD)

    block_r, block_c = iota((block, block), 0), iota((block, block), 1)
    high_r, low_r = block_r // tokens, lax.rem(block_r, tokens)
    high_c, low_c = block_c // tokens, lax.rem(block_c, tokens)
    turn = one(jnp.logical_and(high_r == low_c, low_r == high_c)).astype(BF16)
    by_low = one(lax.rem(iota((block, tokens), 0), tokens) == iota((block, tokens), 1)).astype(BF16)
    expert_r = lax.rem(iota((block, HEAD), 0) // tokens + exp, experts)
    by_slot = [
        one(iota((block, HEAD), 1) == expert_r + s * experts).astype(BF16) for s in range(SLOTS)
    ]
    weight = route_ref[0:1, :] * take0 + route_ref[1:2, :] * take1
    weight_high = weight.astype(BF16)
    weight_low = (weight - weight_high.astype(F32)).astype(BF16)
    for part, piece in enumerate((weight_high, weight_low)):
        spread_out = dot(by_low, piece, ((1,), (1,))).astype(BF16)
        for s in range(SLOTS):
            placed = dot(spread_out, by_slot[s], ((1,), (1,)))
            comb[s, part] = jnp.where(high_r == low_c, placed, 0.0).astype(BF16)
    residual_rows = jnp.concatenate(
        [residual_ref[:, j * width : (j + 1) * width] for j in range(experts)], axis=0
    )
    for s in range(SLOTS):
        chosen = dot(by_slot[s], own_taken, ((1,), (1,))).astype(BF16)
        chosen = dot(chosen, by_low, ((1,), (1,)))
        chosen = jnp.where(low_r == high_c, chosen, 0.0).astype(BF16)
        packed_res[s] = dot(chosen, residual_rows).astype(BF16).reshape(experts, tokens, width)

    pl.semaphore_wait(barrier, experts - 1 + spans - 1)

    total_mine = total_buf.at[ctx]
    for step in range(1, spans):
        remote(total_mine, total_mine, total_sem.at[0], total_sem.at[1], along_ctx(step)).start()
    stages = []

    def exchange(source, target, first):
        copies = []
        for step in (1, 3, 2):
            for h in range(heads):
                k = 3 * h + step - 1 + (0 if first else 3 * heads)
                on_y = (h % 2 == 0) == first
                to = along_y(step) if on_y else along_x(step)
                copies.append(
                    remote(
                        source(h, step), target(h, RING - step), state_send.at[k],
                        state_recv.at[k], to,
                    )
                )
        for copy in copies:
            copy.start()
        stages.extend(copies)
        return copies

    stage1 = exchange(lambda h, q: state_buf.at[0, h], lambda h, q: state_buf.at[q, h], True)

    taken_mine = taken.at[exp]
    for step in range(1, experts):
        remote(taken_mine, taken_mine, taken_sem.at[0], taken_sem.at[1], along_exp(step)).start()

    def cross(source, target, send, recv):
        for step in far_first:
            remote(
                source.at[step], target.at[experts - step], send, recv, along_exp(step)
            ).start()
        pltpu.make_async_copy(source.at[0], target.at[0], recv).start()

    def send_residual(s):
        cross(packed_res.at[s], arrived_res.at[s], res_send.at[s], res_recv.at[s])

    send_residual(0)
    send_residual(1)
    send_residual(2)

    others = total_buf.at[1:]
    arrive(others, total_sem.at[1])
    rows4 = RING * RING
    rho = iota((heads * rows4, spans * 8), 0)
    span_m, head_m = iota((heads * rows4, spans * 8), 1) // 8, lax.rem(
        iota((heads * rows4, spans * 8), 1), 8
    )

    def spans_of(index):
        h = index // rows4
        target, source = lax.rem(index, rows4) // RING, lax.rem(index, RING)
        x_t, y_t = lax.rem(row + target, RING) * RING + col, row * RING + lax.rem(col + target, RING)
        x_s, y_s = lax.rem(row + source, RING) * RING + col, row * RING + lax.rem(col + source, RING)
        return h, jnp.where(h == 0, x_t, y_t), jnp.where(h == 0, y_s, x_s)

    h_r, to_r, from_r = spans_of(rho)
    between = jnp.logical_and(jnp.logical_and(from_r < span_m, span_m < to_r), head_m == h_r)
    log_weight = dot(one(between), total_buf[...].reshape(spans * 8, HEAD), precision=HIGHEST)
    _, to_w, from_w = spans_of(iota((heads * rows4, HEAD), 0))
    span_weight = jnp.where(from_w < to_w, jnp.exp(log_weight), 0.0)

    for copy in stage1:
        copy.wait_recv()
    incoming = []
    for h in range(heads):
        states = [state_buf[q, h].astype(F32) for q in range(RING)]
        for target in (1, 3, 2, 0):
            at = h * rows4 + target * RING
            value = span_weight[at : at + 1, :] * states[0]
            for q in range(1, RING):
                value = value + span_weight[at + q : at + q + 1, :] * states[q]
            if target == 0:
                incoming.append(value)
            else:
                message[target, h] = value.astype(BF16)
    stage2 = exchange(lambda h, q: message.at[q, h], lambda h, q: message_in.at[q, h], False)

    others = taken.at[1:]
    arrive(others, taken_sem.at[1])
    all_taken = taken[...].reshape(block, HEAD)
    owner_r = lax.rem(high_r + low_r + exp, experts)
    picks = []
    for s in range(SLOTS):
        chosen = dot(by_slot[s], all_taken, ((1,), (1,)))
        picks.append(jnp.where(owner_r == high_c, chosen, 0.0).astype(BF16))

    for copy in stage2:
        copy.wait_recv()

    for h in range(heads):
        lanes = slice(h * HEAD, (h + 1) * HEAD)
        state = incoming[h]
        for q in range(1, RING):
            state = state + message_in[q, h].astype(F32)
        carried = dot(query_ref[:, lanes], state.astype(BF16))
        raw = jnp.exp(cum[:, h : h + 1]) * carried + within[:, lanes]
        scale = lax.rsqrt(jnp.mean(raw * raw, axis=-1, keepdims=True) + EPSILON)
        head_out[:, lanes] = (raw * scale * attn_gain_ref[:, lanes]).astype(BF16)

    def send_columns(s):
        packed[s] = dot(picks[s], head_out[...]).astype(BF16).reshape(experts, tokens, width)
        for step in far_first:
            remote(
                packed.at[s, step], arrived.at[s, exp], dispatch_send.at[s], dispatch_recv.at[s],
                along_exp(step),
            ).start()
        pltpu.make_async_copy(packed.at[s, 0], arrived.at[s, exp], dispatch_recv.at[s]).start()

    def token_rows(device):
        return head_out.at[pl.ds(pl.multiple_of(device * tokens, tokens), tokens), :]

    def send_owners():
        for step in far_first:
            to = along_exp(step)
            remote(
                token_rows(to["exp"]), head_recv.at[exp], head_sem.at[0], head_sem.at[1], to
            ).start()
        pltpu.make_async_copy(token_rows(exp), head_recv.at[exp], head_sem.at[1]).start()

    def take_rows(s):
        arrive(arrived_res.at[s], res_recv.at[s])
        turned = dot(turn, arrived_res[s].reshape(block, width))
        arrive(arrived.at[s], dispatch_recv.at[s])
        squares = jnp.zeros((tokens, width), F32)
        rows = []
        for j in range(experts):
            value = turned[j * tokens : (j + 1) * tokens, :] + arrived[s, j].astype(F32)
            rows.append(value)
            squares = squares + value * value
        scale = lax.rsqrt(jnp.sum(squares, axis=-1, keepdims=True) / model + EPSILON)
        for j in range(experts):
            lanes = slice(j * width, (j + 1) * width)
            gathered[s, 0, 0, :, lanes] = (rows[j] * scale * moe_gain_ref[:, lanes]).astype(BF16)

    def columns(n, part=None):
        if part is None:
            return slice(n * half, (n + 1) * half)
        start = n * half + part * quarter
        return slice(start, start + quarter)

    def gather_ring(s, phase, n):
        on_x = (phase == 0) == (n == 0)
        step_by = along_x if on_x else along_y

        def view(part, slot):
            if phase == 0:
                at = (slot, 0) if on_x else (0, slot)
                return gathered.at[s, at[0], at[1], :, columns(n, part)]
            return blocks_view(slice(2 * part, 2 * part + 2), slot)

        def blocks_view(blocks, slot):
            if on_x:
                return gathered.at[s, slot, blocks, :, columns(n)]
            return gathered.at[s, blocks, slot, :, columns(n)]

        k = (s * 2 + phase) * 2 + n

        if phase == 0 and s in DIRECT_GATHER:
            return [
                remote(
                    view(None, 0), view(None, RING - step), ag_send.at[k, step],
                    ag_recv.at[k, step], step_by(step),
                )
                for step in (1, 3, 2)
            ]

        def make(i, part, source, target, step):
            return remote(
                view(part, source), view(part, target), ag_send.at[k, i], ag_recv.at[k, i],
                step_by(step),
            )

        def make_block(i, block, target, step):
            return remote(
                blocks_view(block, 0), blocks_view(block, target), ag_send.at[k, i],
                ag_recv.at[k, i], step_by(step),
            )

        early = phase == 1 and s in EARLY
        return [
            make_block(0, 1, 3, 1) if early else make(0, 0, 0, 3, 1),
            make(1, 1, 0, 1, 3),
            make(2, 1, 0, 3, 1),
            make_block(3, 1, 1, 3) if early else make(3, 0, 0, 1, 3),
            make(4, 0, 3, 2, 1),
            make(5, 1, 1, 2, 3),
        ] + ([make_block(6, 0, 3, 1), make_block(7, 0, 1, 3)] if early else [])

    gathers = {
        (s, phase): [gather_ring(s, phase, n) for n in range(2)]
        for s in range(SLOTS)
        for phase in range(2)
    }

    def gather_early(s):
        for i in (6, 7):
            for ring in gathers[s, 1]:
                ring[i].start()

    def gather_start(s, phase):
        for i in range(4):
            for ring in gathers[s, phase]:
                if i < len(ring):
                    ring[i].start()

    def gather_forward(s, phase):
        if len(gathers[s, phase][0]) < 6:
            return
        for i in range(2):
            for ring in gathers[s, phase]:
                ring[i].wait_recv()
                if i == 0 and len(ring) > 6:
                    ring[6].wait_recv()
                ring[4 + i].start()

    def gather_finish(s, phase):
        for ring in gathers[s, phase]:
            for copy in ring if len(ring) < 6 else ring[2:6] + ring[7:]:
                copy.wait_recv()

    def sum_ring(s, phase, n):
        on_x = (phase == 0) == (n == 1)
        step_by = along_x if on_x else along_y

        def own_view(part, slot):
            if phase == 0:
                two = slice(2 * part, 2 * part + 2)
                if on_x:
                    return partial.at[s, slot, two, :, columns(n)]
                return partial.at[s, two, slot, :, columns(n)]
            at = (slot, 0) if on_x else (0, slot)
            return partial.at[s, at[0], at[1], :, columns(n, part)]

        def opposite(part):
            if phase == 0:
                return opp1.at[s, n, part]
            return opp2.at[s, n, part]

        def final(side, part):
            if phase == 0:
                return fin1.at[s, n, side, 2 * part : 2 * part + 2]
            return fin2.at[s, n, side, :, part * quarter : (part + 1) * quarter]

        k = (s * 2 + phase) * 2 + n

        if phase == 1 and s in DIRECT_SUM:
            copies = [
                remote(
                    own_view(None, step), fin_direct.at[s, n, RING - step], rs_send.at[k, step],
                    rs_recv.at[k, step], step_by(step),
                )
                for step in (2, 1, 3)
            ]
            return copies, own_view, opposite, final

        def make(i, source, target, step):
            return remote(source, target, rs_send.at[k, i], rs_recv.at[k, i], step_by(step))

        copies = [
            make(0, own_view(0, 2), opposite(0), 1),
            make(1, own_view(1, 2), opposite(1), 3),
            make(2, own_view(1, 1), final(0, 1), 1),
            make(3, own_view(0, 3), final(1, 0), 3),
            make(4, own_view(0, 1), final(0, 0), 1),
            make(5, own_view(1, 3), final(1, 1), 3),
        ]
        return copies, own_view, opposite, final

    sums = {
        (s, phase): [sum_ring(s, phase, n) for n in range(2)]
        for s in range(SLOTS)
        for phase in range(2)
    }

    def sum_forward(s, phase):
        if len(sums[s, phase][0][0]) < 6:
            return
        for part, slot in ((0, 1), (1, 3)):
            for copies, own_view, opposite, _ in sums[s, phase]:
                copies[part].wait_recv()
                mine = own_view(part, slot)
                mine[...] = (mine[...].astype(F32) + opposite(part)[...].astype(F32)).astype(BF16)
                copies[4 + part].start()

    def sum_finish(s, phase):
        for n, (copies, own_view, _, final) in enumerate(sums[s, phase]):
            if len(copies) < 6:
                for copy in copies:
                    copy.wait_recv()
                mine = own_view(None, 0)
                value = mine[...].astype(F32)
                for q in range(1, RING):
                    value = value + fin_direct[s, n, q].astype(F32)
                mine[...] = value.astype(BF16)
                continue
            for i in range(2, 6):
                copies[i].wait_recv()
            for part in range(2):
                mine = own_view(part, 0)
                mine[...] = (
                    mine[...].astype(F32)
                    + final(0, part)[...].astype(F32)
                    + final(1, part)[...].astype(F32)
                ).astype(BF16)
            if phase == 0:
                for copy in sums[s, 1][n][0][:4]:
                    copy.start()

    def give_back(s):
        rows = jnp.concatenate(
            [partial[s, 0, 0, :, j * width : (j + 1) * width] for j in range(experts)], axis=0
        )
        back[s] = dot(turn, rows).astype(BF16).reshape(experts, tokens, width)
        cross(back.at[s], returned.at[s], return_send.at[s], return_recv.at[s])

    many = RING * RING * tokens

    def expert_gate(s):
        return dot(gu_weight[0:hid], gathered[s].reshape(many, model), ((1,), (1,)))

    def expert_up(s, gate):
        up = dot(gu_weight[hid : 2 * hid], gathered[s].reshape(many, model), ((1,), (1,)))
        return (jax.nn.silu(gate) * up).astype(BF16)

    def expert_out(s, act):
        for n in range(2):
            for piece in (2 * n, 2 * n + 1):
                lanes = slice(piece * quarter, (piece + 1) * quarter)
                made = dot(act, down_weight[:, lanes], ((0,), (0,)))
                partial[s, :, :, :, lanes] = made.astype(BF16).reshape(
                    RING, RING, tokens, quarter
                )
            for i in range(4):
                sums[s, 0][n][0][i].start()

    send_columns(0)
    send_columns(1)
    send_columns(2)

    def own_rows():
        arrive(head_recv, head_sem.at[1])
        for j in range(experts):
            lanes = slice(j * width, (j + 1) * width)
            hidden[j * tokens : (j + 1) * tokens, :] = (
                residual_ref[:, lanes].astype(F32) + head_recv[j].astype(F32)
            )

    def combine(s):
        arrive(returned.at[s], return_recv.at[s])
        rows = returned[s].reshape(block, width)
        hidden[...] += dot(comb[s, 0], rows) + dot(comb[s, 1], rows)

    def gathers_left(s):
        for phase in range(2):
            for ring in gathers[s, phase]:
                for copy in ring:
                    copy.wait_send()
        arrive(arrived_res.at[s, 1:], res_send.at[s])
        arrive(arrived.at[s, 1:], dispatch_send.at[s])

    def sums_left(s, phase):
        for ring in sums[s, phase]:
            for copy in ring[0]:
                copy.wait_send()

    def first_left():
        for copy in stages:
            copy.wait_send()
        arrive(total_buf.at[1:], total_sem.at[0])
        arrive(taken.at[1:], taken_sem.at[0])
        arrive(head_recv.at[1:], head_sem.at[0])

    take_rows(0)
    gather_start(0, 0)
    gather_early(0)
    send_owners()
    gather_finish(0, 0)
    gather_start(0, 1)
    take_rows(1)
    gather_start(1, 0)
    gather_early(1)
    take_rows(2)
    gather_forward(1, 0)
    gather_forward(0, 1)
    gather_finish(1, 0)
    gather_start(1, 1)
    gather_start(2, 0)
    gather_early(2)
    gather_finish(0, 1)
    for copy in weights:
        copy.wait()
    gate = expert_gate(0)
    gather_forward(1, 1)
    act = expert_up(0, gate)
    gather_forward(2, 0)
    gather_finish(2, 0)
    gather_start(2, 1)
    expert_out(0, act)
    gather_finish(1, 1)
    gate = expert_gate(1)
    gather_forward(2, 1)
    act = expert_up(1, gate)
    sum_forward(0, 0)
    expert_out(1, act)
    gather_finish(2, 1)
    sum_finish(0, 0)
    gate = expert_gate(2)
    sum_forward(1, 0)
    act = expert_up(2, gate)
    sum_forward(0, 1)
    expert_out(2, act)
    sum_finish(0, 1)
    give_back(0)
    first_left()
    own_rows()
    sum_finish(1, 0)
    sum_forward(2, 0)
    sum_forward(1, 1)
    sum_finish(1, 1)
    give_back(1)
    for s in range(SLOTS):
        gathers_left(s)
    combine(0)
    sum_finish(2, 0)
    for s in range(SLOTS - 1):
        sums_left(s, 0)
        sums_left(s, 1)
    arrive(returned.at[0, 1:], return_send.at[0])
    sum_finish(2, 1)
    give_back(2)
    combine(1)
    arrive(returned.at[1, 1:], return_send.at[1])
    sums_left(2, 0)
    sums_left(2, 1)

    arrive(returned.at[2], return_recv.at[2])
    rows = returned[2].reshape(block, width)
    result = (hidden[...] + dot(comb[2, 0], rows) + dot(comb[2, 1], rows)).astype(BF16)
    for j in range(experts):
        out_ref[:, j * width : (j + 1) * width] = result[j * tokens : (j + 1) * tokens, :]
    arrive(returned.at[2, 1:], return_send.at[2])


def body(
    residual_in,
    query_rows,
    key_rows,
    value_rows,
    log_decay,
    attn_gain,
    moe_gain,
    expert_ids,
    route_weight,
    gate_weight,
    up_weight,
    down_weight,
):
    experts = lax.axis_size("exp")
    tokens, model = residual_in.shape
    length, width = query_rows.shape
    heads = width // HEAD
    hid = down_weight.shape[1]
    half, quarter = model // 2, model // 4
    block = experts * tokens
    dma = pltpu.SemaphoreType.DMA
    vmem = pl.BlockSpec(memory_space=pltpu.VMEM)
    hbm = pl.BlockSpec(memory_space=pl.ANY)
    return pl.pallas_call(
        functools.partial(layer_kernel, experts),
        out_shape=jax.ShapeDtypeStruct((tokens, model), BF16),
        in_specs=[hbm] * 12,
        out_specs=vmem,
        scratch_shapes=[
            pltpu.VMEM((tokens, model), BF16),
            pltpu.VMEM((length, width), BF16),
            pltpu.VMEM((length, width), BF16),
            pltpu.VMEM((length, width), BF16),
            pltpu.VMEM((heads, length), F32),
            pltpu.VMEM((1, width), F32),
            pltpu.VMEM((1, model), F32),
            pltpu.VMEM((2, tokens), jnp.int32),
            pltpu.VMEM((2, tokens), F32),
            pltpu.VMEM((RING * RING, 8, HEAD), F32),
            pltpu.VMEM((RING, heads, HEAD, HEAD), BF16),
            pltpu.VMEM((RING, heads, HEAD, HEAD), BF16),
            pltpu.VMEM((RING, heads, HEAD, HEAD), BF16),
            pltpu.VMEM((length, width), F32),
            pltpu.VMEM((length, width), BF16),
            pltpu.VMEM((experts, tokens, width), BF16),
            pltpu.VMEM((block, width), F32),
            pltpu.VMEM((experts, tokens, HEAD), BF16),
            pltpu.VMEM((SLOTS, 2, block, block), BF16),
            pltpu.VMEM((SLOTS, experts, tokens, width), BF16),
            pltpu.VMEM((SLOTS, experts, tokens, width), BF16),
            pltpu.VMEM((SLOTS, experts, tokens, width), BF16),
            pltpu.VMEM((SLOTS, experts, tokens, width), BF16),
            pltpu.VMEM((SLOTS, RING, RING, tokens, model), BF16),
            pltpu.VMEM((SLOTS, RING, RING, tokens, model), BF16),
            pltpu.VMEM((SLOTS, 2, 2, 2, tokens, half), BF16),
            pltpu.VMEM((SLOTS, 2, 2, RING, tokens, half), BF16),
            pltpu.VMEM((SLOTS, 2, 2, tokens, quarter), BF16),
            pltpu.VMEM((SLOTS, 2, 2, tokens, half), BF16),
            pltpu.VMEM((SLOTS, 2, RING, tokens, half), BF16),
            pltpu.VMEM((SLOTS, experts, tokens, width), BF16),
            pltpu.VMEM((SLOTS, experts, tokens, width), BF16),
            pltpu.VMEM((2 * hid, model), BF16),
            pltpu.VMEM((hid, model), BF16),
            dma((9,)),
            dma((3,)),
            dma((2,)),
            dma((2,)),
            dma((6 * heads,)),
            dma((6 * heads,)),
            dma((2,)),
            dma((SLOTS,)),
            dma((SLOTS,)),
            dma((SLOTS,)),
            dma((SLOTS,)),
            dma((SLOTS,)),
            dma((SLOTS,)),
            dma((4 * SLOTS, 8)),
            dma((4 * SLOTS, 8)),
            dma((4 * SLOTS, 6)),
            dma((4 * SLOTS, 6)),
        ],
        compiler_params=pltpu.CompilerParams(
            collective_id=0, has_side_effects=True, vmem_limit_bytes=56 * 1024 * 1024
        ),
    )(
        residual_in,
        query_rows,
        key_rows,
        value_rows,
        log_decay.T,
        attn_gain.reshape(1, -1),
        moe_gain.reshape(1, -1),
        expert_ids.T,
        route_weight.T,
        gate_weight[0].T,
        up_weight[0].T,
        down_weight,
    )


def solution(mesh):
    in_specs = (
        P(("ctx", "exp"), None),
        P("ctx", "exp"),
        P("ctx", "exp"),
        P("ctx", "exp"),
        P("ctx", "exp"),
        P("exp"),
        P(),
        P(("ctx", "exp"), None),
        P(("ctx", "exp"), None),
        P("exp", None, "ctx"),
        P("exp", None, "ctx"),
        P("exp", "ctx", None),
    )
    out_specs = P(("ctx", "exp"), None)
    return jax.shard_map(body, mesh=mesh, in_specs=in_specs, out_specs=out_specs, check_vma=False)
```
